256 devices in a mesh: seg: 8 (over x, core), dom: 32 (over z, y).
Axes of the slice: x: 4, y: 4, z: 8, core: 2. Of those that a mesh axis runs over, the one named last changes fastest.
Arguments:
- element_state: float32 [180, 393216], P(None, ('seg', 'dom')), may hold values from -6 to 6
- face_source: int32 [4, 393216], P(None, ('seg', 'dom')), may hold values from 0 to 10239, as said below
- send_faces: int32 [32, 32768], P(None, ('seg', 'dom')), may hold values from 0 to 6143
- plus_faces: int32 [32768], P(('seg', 'dom')), may hold values from 0 to 6143, as said below
- minus_faces: int32 [32768], P(('seg', 'dom')), may hold values from 0 to 6143
- fault_count: int32 [256], P(('seg', 'dom')), may hold values from 1 to 128, as said below
- normal_stress: float32 [16, 32768], P(None, ('seg', 'dom')), may hold values from 1 to 10
- state_variable: float32 [16, 32768], P(None, ('seg', 'dom')), may hold values from 0.5 to 3
- geometry: float32 [3, 393216], P(None, ('seg', 'dom')), may hold values from 0.3 to 3
- face_area: float32 [4, 393216], P(None, ('seg', 'dom')), may hold values from 0.5 to 4
- restriction: bfloat16 [120, 180], replicated, may hold values from -0.4375 to 0.4375
- volume_ops: bfloat16 [540, 180], replicated, may hold values from -0.4375 to 0.4375
- lift_operator: bfloat16 [180, 120], replicated, may hold values from -0.5 to 0.5
- to_points: float32 [16, 10], replicated, may hold values from -2 to 2
- to_nodes: float32 [10, 16], replicated, may hold values from -1.5 to 1.5
Outputs:
- element_state_next: float32 [180, 393216], P(None, ('seg', 'dom'))
- fault_slip: float32 [16, 32768], P(None, ('seg', 'dom'))
The draws below stay inside these ranges and needn't reach their ends.
Inputs may be any that keep to these rules, and one draw needn't show every extreme that they name: `face_source`: on each partition every received slot is named exactly once; fault faces are never named. On each partition plus_faces and minus_faces are all different faces. `fault_count`: some owner has all 128 slots live.
All inputs are finite; a program needn't handle non-finite values.
Results may differ from the reference program's by a relative error of at most 0.0042.
Values may be sent and summed in bfloat16 or wider, within the bound.
No kernel may reach another device: no remote copies, remote signals or barrier semaphores. Data moves between devices by JAX's collectives and lax.ppermute only.
A program may use at most 64 MiB of HBM per device.

```python
import math
import jax
import jax.numpy as jnp
from jax import lax

VALUES = 180
TRACE = 30
FACE_NODES = 10
POINTS = 16
STEPS = 2
NEWTON = 4
ELEM_DEV = 1536
SEND_SLOTS = 128
FAULT_DEV = 128
N_ELEM = 393216
N_FAULT = 32768
N_SEND = 32768
N_SEG = 8
N_DOM = 32


def face_orders(key):
    devices = N_SEG * N_DOM
    device_keys = jax.random.split(key, devices)
    return jax.vmap(lambda single: jax.random.permutation(single, 4 * ELEM_DEV))(device_keys)


def draw_face_source(key, part):
    orders = face_orders(key)
    key = jax.random.fold_in(key, 11)
    devices = N_SEG * N_DOM
    faces = 4 * ELEM_DEV
    first = 2 * FAULT_DEV
    position = jax.vmap(lambda order: jnp.zeros((faces,), jnp.int32).at[order].set(jnp.arange(faces, dtype=jnp.int32)))(orders)
    offset = jax.random.randint(key, (devices, faces), 0, faces - first)
    local_face = jnp.take_along_axis(orders, first + offset, axis=1)
    in_halo = (position >= first) & (position < first + N_DOM * SEND_SLOTS)
    chosen = jnp.where(in_halo, faces + position - first, local_face).astype(jnp.int32)
    chosen = chosen.reshape(devices, 4, ELEM_DEV)
    return jnp.transpose(chosen, (1, 0, 2)).reshape(4, devices * ELEM_DEV)


def draw_plus_faces(key, part):
    orders = face_orders(key)
    return orders[:, :FAULT_DEV].reshape(-1).astype(jnp.int32)


def draw_minus_faces(key, part):
    orders = face_orders(key)
    return orders[:, FAULT_DEV:2 * FAULT_DEV].reshape(-1).astype(jnp.int32)


def draw_fault_count(key, part):
    key = jax.random.fold_in(key, 13)
    devices = N_SEG * N_DOM
    first_key, second_key = jax.random.split(key)
    divisor = jax.random.randint(first_key, (devices,), 1, 5)
    counts = FAULT_DEV // divisor
    chosen = jax.random.randint(second_key, (), 0, devices)
    return counts.at[chosen].set(FAULT_DEV).astype(jnp.int32)


def with_ends(result, key, low, top_value):
    place = [jax.random.randint(jax.random.fold_in(key, axis), (), 0, length) for axis, length in enumerate(result.shape)]
    main_axis = result.shape.index(max(result.shape))
    neighbour = place[:main_axis] + [(place[main_axis] + 1) % result.shape[main_axis]] + place[main_axis + 1:]
    return result.at[tuple(place)].set(low).at[tuple(neighbour)].set(top_value)


def levels(own_key, dims, cuts, least, top_value):
    def one(dim, shards_of):
        heights = jax.random.uniform(jax.random.fold_in(jax.random.fold_in(own_key, 6), dim), (shards_of,), jnp.float32, least / len(cuts), top_value / len(cuts))
        return jnp.repeat(jnp.exp(heights), dims[dim] // shards_of).reshape((-1,) + (1,) * (len(dims) - dim - 1))

    level = one(*cuts[0])
    for cut in cuts[1:]:
        level = level * one(*cut)
    return level


def scatter_about(key, dims, deviation, reach, pieces=(), kind=jnp.bfloat16):
    level = levels(key, dims, pieces, -0.22, 0.18) if pieces else 1.0
    values = jax.random.normal(key, dims, jnp.float32) * deviation * level
    return jnp.minimum(jnp.maximum(values, -reach), reach).astype(kind)


def setup_inputs(seed: int = 0) -> dict:
    keys = jax.random.split(jax.random.key(seed), 16)
    return {
        "element_state": scatter_about(keys[0], (VALUES, N_ELEM), 1.0, 6.0, ((1, 256),), jnp.float32),
        "face_source": draw_face_source(jax.random.fold_in(keys[15], 71), 0),
        "send_faces": with_ends(jax.random.randint(keys[2], (N_DOM, N_SEND), 0, 4 * ELEM_DEV), jax.random.fold_in(keys[2], 1), 0, (4 * ELEM_DEV) - 1).astype(jnp.int32),
        "plus_faces": draw_plus_faces(jax.random.fold_in(keys[15], 71), 0),
        "minus_faces": draw_minus_faces(jax.random.fold_in(keys[15], 71), 0),
        "fault_count": draw_fault_count(jax.random.fold_in(keys[15], 71), 0),
        "normal_stress": jnp.clip(jnp.exp(math.log(10.0) - 2.3025851 * jax.random.uniform(keys[6], (POINTS, N_FAULT), jnp.float32) ** levels(keys[6], (POINTS, N_FAULT), ((1, 256),), -0.2, 0.2)), 1.0, 10.0),
        "state_variable": jnp.clip(0.5 + 2.5 * jax.random.uniform(keys[7], (POINTS, N_FAULT), jnp.float32) ** levels(keys[7], (POINTS, N_FAULT), ((1, 256),), -0.2, 0.2), 0.5, 3.0),
        "geometry": jnp.clip(jnp.exp(math.log(3.0) - 2.3025851 * jax.random.uniform(keys[8], (3, N_ELEM), jnp.float32) ** levels(keys[8], (3, N_ELEM), ((1, 256),), -0.2, 0.2)), 0.3, 3.0),
        "face_area": jnp.clip(jnp.exp(math.log(4.0) - 2.0794415 * jax.random.uniform(keys[9], (4, N_ELEM), jnp.float32) ** levels(keys[9], (4, N_ELEM), ((1, 256),), -0.2, 0.2)), 0.5, 4.0),
        "restriction": scatter_about(keys[10], (4 * TRACE, VALUES), VALUES ** -0.5, 0.4375),
        "volume_ops": scatter_about(keys[11], (3 * VALUES, VALUES), VALUES ** -0.5, 0.4375),
        "lift_operator": scatter_about(keys[12], (VALUES, 4 * TRACE), (4 * TRACE) ** -0.5, 0.5),
        "to_points": scatter_about(keys[13], (POINTS, FACE_NODES), FACE_NODES ** -0.5, 2.0, (), jnp.float32),
        "to_nodes": scatter_about(keys[14], (FACE_NODES, POINTS), POINTS ** -0.5, 1.5, (), jnp.float32),
    }


IMPEDANCE = 1.0
FRICTION_A = 0.2
REGULARIZE = 0.25
TIME_STEP = 0.25

def inverse_sinh(value):
    return jnp.log(value + jnp.sqrt(value * value + 1.0))

def friction(plus_side, minus_side, normal_stress, state_variable, to_points, to_nodes):
    difference = plus_side.astype(jnp.float32) - minus_side.astype(jnp.float32)
    difference = difference.reshape(3, to_points.shape[1], -1)
    at_points = jnp.einsum('qn,cnf->cqf', to_points, difference, precision=lax.Precision.HIGHEST)
    magnitude = jnp.sqrt(at_points[1] * at_points[1] + at_points[2] * at_points[2] + REGULARIZE)
    rate_scale = 0.5 * jnp.exp(state_variable)
    slip_rate = jnp.zeros_like(magnitude)
    for sweep in range(NEWTON):
        scaled_rate = slip_rate * rate_scale
        residual_value = IMPEDANCE * (magnitude - slip_rate) - normal_stress * FRICTION_A * inverse_sinh(scaled_rate)
        derivative = IMPEDANCE + normal_stress * FRICTION_A * rate_scale / jnp.sqrt(1.0 + scaled_rate * scaled_rate)
        slip_rate = slip_rate + residual_value / derivative
    slip_share = slip_rate / magnitude
    point_jump = jnp.stack([at_points[0], at_points[1] * slip_share, at_points[2] * slip_share])
    nodal_jump = jnp.einsum('nq,cqf->cnf', to_nodes, point_jump, precision=lax.Precision.HIGHEST)
    return (nodal_jump.reshape(-1, nodal_jump.shape[-1]), slip_rate)

def advance_local(element_state, face_jump, geometry, face_area, volume_ops, lift_operator):
    elements = element_state.shape[1]
    packed = element_state.astype(jnp.bfloat16)
    scaled_jump = (face_jump.reshape(-1, 4, elements) * face_area[None]).reshape(-1, elements).astype(jnp.bfloat16)
    lifted = jnp.dot(lift_operator, scaled_jump, preferred_element_type=jnp.float32)
    volume = jnp.dot(volume_ops, packed, preferred_element_type=jnp.float32).reshape(3, -1, elements)
    volume = lax.optimization_barrier(jnp.sum(volume * geometry[:, None, :], axis=0))
    return element_state + TIME_STEP * (volume - lifted)

def by_device(array, devices):
    shaped = array.reshape(array.shape[:-1] + (devices, array.shape[-1] // devices))
    return jnp.moveaxis(shaped, -2, 0)

def from_device(array):
    moved = jnp.moveaxis(array, 0, -2)
    return moved.reshape(moved.shape[:-2] + (-1,))

def along_seg(array, amount):
    shaped = array.reshape((N_SEG, N_DOM) + array.shape[1:])
    return jnp.roll(shaped, amount, axis=0).reshape(array.shape)

def reference(element_state, face_source, send_faces, plus_faces, minus_faces, fault_count, normal_stress, state_variable, geometry, face_area, restriction, volume_ops, lift_operator, to_points, to_nodes):
    devices = N_SEG * N_DOM
    elements = by_device(element_state, devices)
    sources = by_device(face_source, devices).reshape(devices, -1)
    sending = by_device(send_faces, devices).reshape(devices, -1)
    plus_list = by_device(plus_faces, devices)
    minus_list = by_device(minus_faces, devices)
    counts = fault_count.reshape(-1)
    stresses = by_device(normal_stress, devices)
    variables = by_device(state_variable, devices)
    geometries = by_device(geometry, devices)
    areas = by_device(face_area, devices)
    slots = plus_list.shape[1]
    is_live = jnp.arange(slots, dtype=jnp.int32)[None, :] < counts[:, None]
    live_back = along_seg(is_live, -1)
    slip_out = jnp.zeros_like(stresses)
    for step in range(STEPS):

        def face_traces(local_state):
            packed = local_state.astype(jnp.bfloat16)
            made = jnp.dot(restriction, packed, preferred_element_type=jnp.float32).astype(jnp.bfloat16)
            return made.reshape(TRACE, -1)
        traces = lax.map(face_traces, elements)
        outgoing = jax.vmap(lambda table, picks: table[:, picks])(traces, sending)
        outgoing = outgoing.reshape(N_SEG, N_DOM, TRACE, N_DOM, SEND_SLOTS)
        received = jnp.transpose(outgoing, (0, 3, 2, 1, 4)).reshape(devices, TRACE, N_DOM * SEND_SLOTS)
        trace_pool = jnp.concatenate([traces, received], axis=2)
        exterior = jax.vmap(lambda table, picks: table[:, picks])(trace_pool, sources)
        face_jump = traces.astype(jnp.float32) - exterior.astype(jnp.float32)
        plus_traces = jax.vmap(lambda table, picks: table[:, picks])(traces, plus_list)
        minus_traces = jax.vmap(lambda table, picks: table[:, picks])(traces, minus_list)
        partner = along_seg(minus_traces, 1)
        nodal_jump, slip_rate = jax.vmap(lambda a, b, c, d: friction(a, b, c, d, to_points, to_nodes))(plus_traces, partner, stresses, variables)
        returned = along_seg(nodal_jump, -1)

        def override(jump_table, plus_picks, minus_picks, live_own, live_other, own_jump, other_jump):
            jump_table = jump_table.at[:, plus_picks].set(jnp.where(live_own[None, :], own_jump, jump_table[:, plus_picks]))
            return jump_table.at[:, minus_picks].set(jnp.where(live_other[None, :], -other_jump, jump_table[:, minus_picks]))
        face_jump = jax.vmap(override)(face_jump, plus_list, minus_list, is_live, live_back, nodal_jump, returned)
        elements = lax.map(lambda packs: advance_local(packs[0], packs[1], packs[2], packs[3], volume_ops, lift_operator), (elements, face_jump, geometries, areas))
        slip_out = jnp.where(is_live[:, None, :], slip_rate, 0.0)
    return (from_device(elements), from_device(slip_out))
```

```python
import functools

import jax
import jax.numpy as jnp
from jax import lax
from jax.experimental import pallas as pl
from jax.experimental.pallas import tpu as pltpu
from jax.sharding import PartitionSpec as P

STEPS = 2
NEWTON = 4
IMPEDANCE = 1.0
FRICTION_A = 0.2
REGULARIZE = 0.25
TIME_STEP = 0.25

F32 = jnp.float32
BF16 = jnp.bfloat16

VALUES = 180
TRACE = 30
ROWS = 32
ELEMS = 1536
PEERS = 32
SLOTS = 128
POINTS = 16
NODES = 10
BLOCK = 256
TILES = ELEMS // BLOCK
LOCAL = 4 * TILES
REMOTE = PEERS * SLOTS // BLOCK
FAULTS = 2 * SLOTS
VMEM_LIMIT = 32 * 2**20


def inverse_sinh(value):
    return jnp.log(value + jnp.sqrt(value * value + 1.0))


def row_order():
    row = lax.broadcasted_iota(jnp.int32, (4 * ROWS, 4 * TRACE), 0)
    column = lax.broadcasted_iota(jnp.int32, (4 * ROWS, 4 * TRACE), 1)
    face = lax.shift_right_logical(row, 5)
    value = jnp.bitwise_and(row, ROWS - 1)
    return jnp.where(column == 4 * value + face, 1.0, 0.0).astype(BF16)


def make_traces(packed, restriction, table, traces):
    ordered = jnp.dot(row_order(), restriction, preferred_element_type=F32).astype(BF16)
    made = jnp.dot(ordered, packed, preferred_element_type=F32).astype(BF16)
    if traces is not None:
        traces[...] = made
    for block in range(LOCAL):
        face, tile = divmod(block, TILES)
        table[block * ROWS : (block + 1) * ROWS, :] = made[
            face * ROWS : (face + 1) * ROWS, tile * BLOCK : (tile + 1) * BLOCK
        ]


def pick(table, index, blocks):
    low = jnp.bitwise_and(index, BLOCK - 1)
    high = jnp.broadcast_to(lax.shift_right_logical(index, 8), (ROWS, index.shape[1]))
    lanes = lax.broadcasted_iota(jnp.int32, (BLOCK, index.shape[1]), 0)
    selector = jnp.where(lanes == low, 1.0, 0.0).astype(BF16)
    product = jnp.dot(table[0 : blocks * ROWS, :], selector, preferred_element_type=F32)
    picked = jnp.zeros((ROWS, index.shape[1]), F32)
    for block in range(blocks):
        picked = jnp.where(high == block, product[block * ROWS : (block + 1) * ROWS], picked)
    return picked


def send_traces(table, send_faces, plus_faces, minus_faces, sent, plus_out, minus_out):
    def body(turn, carry):
        faces = send_faces[pl.ds(pl.multiple_of(turn * 8, 8), 8), :]
        for pair in range(4):
            index = jnp.concatenate([faces[2 * pair : 2 * pair + 1], faces[2 * pair + 1 : 2 * pair + 2]], axis=1)
            picked = pick(table, index, LOCAL).astype(BF16)
            sent[turn * 8 + 2 * pair] = picked[:, :SLOTS]
            sent[turn * 8 + 2 * pair + 1] = picked[:, SLOTS:]
        return carry

    index = jnp.concatenate([plus_faces[...], minus_faces[...]], axis=1)
    picked = pick(table, index, LOCAL).astype(BF16)
    plus_out[...] = picked[:, :SLOTS].astype(plus_out.dtype)
    minus_out[...] = picked[:, SLOTS:]
    lax.fori_loop(0, PEERS // 8, body, 0)


def friction(difference, stress, state, to_points, to_nodes, jump):
    weights = [jnp.broadcast_to(to_points[:, n : n + 1], stress.shape) for n in range(NODES)]
    at_points = []
    for component in range(3):
        total = weights[0] * difference[component * NODES : component * NODES + 1]
        for n in range(1, NODES):
            row = component * NODES + n
            total = total + weights[n] * difference[row : row + 1]
        at_points.append(total)
    magnitude = jnp.sqrt(at_points[1] * at_points[1] + at_points[2] * at_points[2] + REGULARIZE)
    rate_scale = 0.5 * jnp.exp(state)
    slip_rate = jnp.zeros_like(magnitude)
    for _ in range(NEWTON):
        scaled_rate = slip_rate * rate_scale
        residual_value = IMPEDANCE * (magnitude - slip_rate) - stress * FRICTION_A * inverse_sinh(scaled_rate)
        derivative = IMPEDANCE + stress * FRICTION_A * rate_scale / jnp.sqrt(1.0 + scaled_rate * scaled_rate)
        slip_rate = slip_rate + residual_value / derivative
    share = slip_rate / magnitude
    point_jump = [at_points[0], at_points[1] * share, at_points[2] * share]
    columns = [jnp.broadcast_to(to_nodes[:, q : q + 1], (NODES, stress.shape[1])) for q in range(POINTS)]
    for component in range(3):
        total = columns[0] * point_jump[component][0:1]
        for q in range(1, POINTS):
            total = total + columns[q] * point_jump[component][q : q + 1]
        jump[component * NODES : (component + 1) * NODES, :] = total
    return slip_rate


def first_kernel(
    element_state, send_faces, plus_faces, minus_faces, fault_count, stress, state_variable, restriction,
    sent, plus_out, minus_out, table,
):
    make_traces(element_state[...].astype(BF16), restriction[...], table, None)
    send_traces(table, send_faces, plus_faces, minus_faces, sent, plus_out.at[0:ROWS, :], minus_out)
    plus_out[ROWS : ROWS + POINTS, :] = stress[...]
    plus_out[ROWS + POINTS : ROWS + 2 * POINTS, :] = state_variable[...]
    plus_out[ROWS + 2 * POINTS :, :] = jnp.full((8, SLOTS), fault_count[0], jnp.int32).astype(F32)


def step_kernel(
    last, element_state, received, partner, next_plus, next_constants, face_source, send_faces, plus_faces, minus_faces,
    own_plus, own_minus, fault_count, stress, state_variable, geometry, face_area, restriction, volume_ops,
    lift_operator, to_points, to_nodes, *rest,
):
    if last:
        state_out, slip_out, table, traces, jump, masked, override, scaled = rest
    else:
        state_out, sent, plus_out, minus_out, table, traces, jump, masked, override, scaled = rest
    packed = element_state[...].astype(BF16)
    make_traces(packed, restriction[...], table, traces)
    for block in range(REMOTE):
        table[(LOCAL + block) * ROWS : (LOCAL + block + 1) * ROWS, :] = jnp.concatenate(
            [received[2 * block], received[2 * block + 1]], axis=1
        )

    plus_side = jnp.concatenate([own_plus[0:ROWS, :].astype(F32), next_plus[0:ROWS, :].astype(F32)], axis=1)
    minus_side = jnp.concatenate([partner[...].astype(F32), own_minus[...].astype(F32)], axis=1)
    both_stress = jnp.concatenate([stress[...], next_constants[ROWS : ROWS + POINTS, :]], axis=1)
    both_state = jnp.concatenate([state_variable[...], next_constants[ROWS + POINTS : ROWS + 2 * POINTS, :]], axis=1)
    slip_rate = friction(plus_side - minus_side, both_stress, both_state, to_points[...], to_nodes[...], jump)
    slot = lax.broadcasted_iota(jnp.int32, (1, SLOTS), 1)
    own_live = slot < fault_count[0]
    next_live = slot.astype(F32) < next_constants[ROWS + 2 * POINTS : ROWS + 2 * POINTS + 1, :]
    sign = jnp.concatenate([jnp.where(own_live, 1.0, 0.0), jnp.where(next_live, -1.0, 0.0)], axis=1)
    if last:
        slip_out[...] = jnp.where(own_live, slip_rate[:, :SLOTS], 0.0)

    row = lax.broadcasted_iota(jnp.int32, (ROWS, FAULTS), 0)
    jump[TRACE : TRACE + 2, :] = jnp.zeros((2, FAULTS), F32)
    values = jnp.where(row < TRACE, jump[...] * sign, jnp.where(row == TRACE, jnp.abs(sign), 0.0))
    coarse = values.astype(BF16).astype(F32)
    parts = jnp.concatenate([coarse, values - coarse], axis=0)
    faces = jnp.concatenate([plus_faces[...], minus_faces[...]], axis=1)
    high = jnp.broadcast_to(lax.shift_right_logical(faces, 8), parts.shape)
    for block in range(LOCAL):
        masked[block * 2 * ROWS : (block + 1) * 2 * ROWS, :] = jnp.where(high == block, parts, 0.0).astype(BF16)
    lanes = lax.broadcasted_iota(jnp.int32, (BLOCK, FAULTS), 0)
    selector = jnp.where(lanes == jnp.bitwise_and(faces, BLOCK - 1), 1.0, 0.0).astype(BF16)
    override[...] = lax.dot_general(masked[...], selector, (((1,), (1,)), ((), ())), preferred_element_type=F32)

    def body(face, carry):
        rows = pl.ds(pl.multiple_of(face * ROWS, ROWS), ROWS)
        for tile in range(TILES):
            columns = slice(tile * BLOCK, (tile + 1) * BLOCK)
            exterior = pick(table, face_source[pl.ds(face, 1), columns], LOCAL + REMOTE)
            start = (face * TILES + tile) * 2 * ROWS
            changed = (
                override[pl.ds(pl.multiple_of(start, ROWS), ROWS), :]
                + override[pl.ds(pl.multiple_of(start + ROWS, ROWS), ROWS), :]
            )
            plain = traces[rows, columns].astype(F32) - exterior
            face_jump = jnp.where(changed[TRACE : TRACE + 1] > 0.5, changed, plain)
            scaled[rows, columns] = (face_jump * face_area[pl.ds(face, 1), columns]).astype(BF16)
        return carry

    lax.fori_loop(0, 4, body, 0)

    ordered = lax.dot_general(
        lift_operator[...], row_order(), (((1,), (1,)), ((), ())), preferred_element_type=F32
    ).astype(BF16)
    change = -jnp.dot(ordered, scaled[...], preferred_element_type=F32)
    operators = volume_ops[...].astype(F32)
    for direction in range(3):
        operator = operators[direction * VALUES : (direction + 1) * VALUES].astype(BF16)
        change = change + jnp.dot(operator, packed, preferred_element_type=F32) * geometry[direction : direction + 1, :]
    state = element_state[...] + TIME_STEP * change
    state_out[...] = state
    if not last:
        make_traces(state.astype(BF16), restriction[...], table, None)
        send_traces(table, send_faces, plus_faces, minus_faces, sent, plus_out, minus_out)


def call(kernel, outs, scratch, smem, *args):
    vmem = pl.BlockSpec(memory_space=pltpu.VMEM)
    return pl.pallas_call(
        kernel,
        out_shape=outs,
        in_specs=[pl.BlockSpec(memory_space=pltpu.SMEM) if i == smem else vmem for i in range(len(args))],
        out_specs=[vmem] * len(outs),
        scratch_shapes=scratch,
        compiler_params=pltpu.CompilerParams(vmem_limit_bytes=VMEM_LIMIT),
    )(*args)


def shards(
    element_state,
    face_source,
    send_faces,
    plus_faces,
    minus_faces,
    fault_count,
    normal_stress,
    state_variable,
    geometry,
    face_area,
    restriction,
    volume_ops,
    lift_operator,
    to_points,
    to_nodes,
):
    segments = lax.axis_size("seg")
    up = [(s, (s + 1) % segments) for s in range(segments)]
    down = [(s, (s - 1) % segments) for s in range(segments)]
    plus_faces = plus_faces.reshape(1, SLOTS)
    minus_faces = minus_faces.reshape(1, SLOTS)
    block = jax.ShapeDtypeStruct((ROWS, SLOTS), BF16)
    sent_shape = jax.ShapeDtypeStruct((PEERS, ROWS, SLOTS), BF16)
    table = pltpu.VMEM(((LOCAL + REMOTE) * ROWS, BLOCK), BF16)
    scratch = [
        table,
        pltpu.VMEM((4 * ROWS, ELEMS), BF16),
        pltpu.VMEM((ROWS, FAULTS), F32),
        pltpu.VMEM((LOCAL * 2 * ROWS, FAULTS), BF16),
        pltpu.VMEM((LOCAL * 2 * ROWS, BLOCK), F32),
        pltpu.VMEM((4 * ROWS, ELEMS), BF16),
    ]
    constants_rows = ROWS + 2 * POINTS + 8
    sent, plus, minus = call(
        first_kernel,
        [sent_shape, jax.ShapeDtypeStruct((constants_rows, SLOTS), F32), block],
        [table],
        4,
        element_state, send_faces, plus_faces, minus_faces, fault_count, normal_stress, state_variable, restriction,
    )
    next_constants = None
    for step in range(STEPS):
        last = step == STEPS - 1
        partner = lax.ppermute(minus, "seg", up)
        next_plus = lax.ppermute(plus, "seg", down)
        if next_constants is None:
            next_constants = next_plus
        received = lax.all_to_all(sent, "dom", 0, 0, tiled=True)
        state_shape = jax.ShapeDtypeStruct(element_state.shape, F32)
        if last:
            outs = [state_shape, jax.ShapeDtypeStruct(normal_stress.shape, F32)]
        else:
            outs = [state_shape, sent_shape, block, block]
        result = call(
            functools.partial(step_kernel, last), outs, scratch, 11,
            element_state, received, partner, next_plus, next_constants, face_source, send_faces, plus_faces, minus_faces,
            plus, minus, fault_count, normal_stress, state_variable, geometry, face_area, restriction, volume_ops,
            lift_operator, to_points, to_nodes,
        )
        if last:
            return tuple(result)
        element_state, sent, plus, minus = result


def solution(mesh):
    placed = (
        P(None, ("seg", "dom")),
        P(None, ("seg", "dom")),
        P(None, ("seg", "dom")),
        P(("seg", "dom")),
        P(("seg", "dom")),
        P(("seg", "dom")),
        P(None, ("seg", "dom")),
        P(None, ("seg", "dom")),
        P(None, ("seg", "dom")),
        P(None, ("seg", "dom")),
        P(),
        P(),
        P(),
        P(),
        P(),
    )
    return jax.shard_map(
        shards,
        mesh=mesh,
        in_specs=placed,
        out_specs=(P(None, ("seg", "dom")), P(None, ("seg", "dom"))),
        check_vma=False,
    )
```

```python
import functools

import jax
import jax.numpy as jnp
from jax import lax
from jax.experimental import pallas as pl
from jax.experimental.pallas import tpu as pltpu
from jax.sharding import PartitionSpec as P

STEPS = 2
NEWTON = 4
IMPEDANCE = 1.0
FRICTION_A = 0.2
REGULARIZE = 0.25
TIME_STEP = 0.25

F32 = jnp.float32
BF16 = jnp.bfloat16

VALUES = 180
TRACE = 30
ROWS = 32
ELEMS = 1536
PEERS = 32
SLOTS = 128
POINTS = 16
NODES = 10
BLOCK = 256
TILES = ELEMS // BLOCK
LOCAL = 4 * TILES
REMOTE = PEERS * SLOTS // BLOCK
FAULTS = 2 * SLOTS
PARTS = 3
VMEM_LIMIT = 32 * 2**20


def inverse_sinh(value):
    return jnp.log(value + jnp.sqrt(value * value + 1.0))


def row_order():
    row = lax.broadcasted_iota(jnp.int32, (4 * ROWS, 4 * TRACE), 0)
    column = lax.broadcasted_iota(jnp.int32, (4 * ROWS, 4 * TRACE), 1)
    face = lax.shift_right_logical(row, 5)
    value = jnp.bitwise_and(row, ROWS - 1)
    return jnp.where(column == 4 * value + face, 1.0, 0.0).astype(BF16)


def make_traces(packed, ordered, table, first, tiles):
    made = jnp.dot(ordered, packed, preferred_element_type=F32).astype(BF16)
    for face in range(4):
        for tile in range(tiles):
            start = (face * TILES + first + tile) * ROWS
            table[start : start + ROWS, :] = made[face * ROWS : (face + 1) * ROWS, tile * BLOCK : (tile + 1) * BLOCK]


def order_rows(restriction):
    return lax.dot_general(
        row_order(), restriction, (((1,), (1,)), ((), ())), preferred_element_type=F32
    ).astype(BF16)


def pick(table, index, first, blocks):
    width = index.shape[1]
    low = jnp.bitwise_and(index, BLOCK - 1)
    high = jnp.broadcast_to(lax.shift_right_arithmetic(index, 8), (8, width))
    lanes = lax.broadcasted_iota(jnp.int32, (BLOCK, width), 0)
    selector = jnp.where(lanes == low, 1.0, 0.0).astype(BF16)
    product = jnp.dot(table[first * ROWS : (first + blocks) * ROWS, :], selector, preferred_element_type=F32)
    product = product.reshape(blocks, ROWS // 8, 8, width)
    picked = jnp.zeros((ROWS // 8, 8, width), F32)
    for block in range(blocks):
        here = jnp.broadcast_to((high == first + block)[None], picked.shape)
        picked = jnp.where(here, product[block], picked)
    return picked.reshape(ROWS, width)


def pick_sent(table, send_faces, plus_faces, minus_faces, sent, plus_out, minus_out, outgoing, sems):
    index = jnp.concatenate([plus_faces[...], minus_faces[...]], axis=1)
    picked = pick(table, index, 0, LOCAL).astype(BF16)
    plus_out[...] = picked[:, :SLOTS]
    minus_out[...] = picked[:, SLOTS:]

    def body(turn, carry):
        start = pl.multiple_of(turn * 8, 8)
        faces = send_faces[pl.ds(start, 8), :]
        for pair in range(4):
            index = jnp.concatenate([faces[2 * pair : 2 * pair + 1], faces[2 * pair + 1 : 2 * pair + 2]], axis=1)
            picked = pick(table, index, 0, LOCAL).astype(BF16)
            outgoing[start + 2 * pair] = picked[:, :SLOTS]
            outgoing[start + 2 * pair + 1] = picked[:, SLOTS:]
        part = pl.ds(start, 8)
        pltpu.make_async_copy(outgoing.at[part], sent.at[part], sems.at[turn]).start()
        return carry

    lax.fori_loop(0, PEERS // 8, body, 0)
    for turn in range(PEERS // 8):
        part = slice(turn * 8, turn * 8 + 8)
        pltpu.make_async_copy(outgoing.at[part], sent.at[part], sems.at[turn]).wait()


def friction(difference, stress, state, to_points, to_nodes, jump):
    weights = [jnp.broadcast_to(to_points[:, n : n + 1], stress.shape) for n in range(NODES)]
    at_points = []
    for component in range(3):
        total = weights[0] * difference[component * NODES : component * NODES + 1]
        for n in range(1, NODES):
            row = component * NODES + n
            total = total + weights[n] * difference[row : row + 1]
        at_points.append(total)
    magnitude = jnp.sqrt(at_points[1] * at_points[1] + at_points[2] * at_points[2] + REGULARIZE)
    rate_scale = 0.5 * jnp.exp(state)
    slip_rate = jnp.zeros_like(magnitude)
    for _ in range(NEWTON):
        scaled_rate = slip_rate * rate_scale
        residual_value = IMPEDANCE * (magnitude - slip_rate) - stress * FRICTION_A * inverse_sinh(scaled_rate)
        derivative = IMPEDANCE + stress * FRICTION_A * rate_scale / jnp.sqrt(1.0 + scaled_rate * scaled_rate)
        slip_rate = slip_rate + residual_value / derivative
    share = slip_rate / magnitude
    point_jump = [at_points[0], at_points[1] * share, at_points[2] * share]
    columns = [jnp.broadcast_to(to_nodes[:, q : q + 1], (NODES, stress.shape[1])) for q in range(POINTS)]
    for component in range(3):
        total = columns[0] * point_jump[component][0:1]
        for q in range(1, POINTS):
            total = total + columns[q] * point_jump[component][q : q + 1]
        jump[component * NODES : (component + 1) * NODES, :] = total
    return slip_rate


def first_kernel(
    element_state, send_faces, plus_faces, minus_faces, stress, state_variable, fault_count, restriction,
    sent, constants, plus_out, minus_out, table,
    state_here, send_here, plus_here, minus_here, restriction_here, outgoing, in_sems, out_sems,
):
    small = [
        (restriction, restriction_here),
        (plus_faces, plus_here),
        (minus_faces, minus_here),
        (send_faces, send_here),
        (stress, constants.at[0:POINTS, :]),
        (state_variable, constants.at[POINTS : 2 * POINTS, :]),
    ]
    copies = [pltpu.make_async_copy(here, there, in_sems.at[i]) for i, (here, there) in enumerate(small)]
    width = ELEMS // PARTS
    for part in range(PARTS):
        columns = slice(part * width, (part + 1) * width)
        copies.append(
            pltpu.make_async_copy(
                element_state.at[:, columns], state_here.at[:, columns], in_sems.at[len(small) + part]
            )
        )
    for copy in copies:
        copy.start()
    constants[2 * POINTS :, :] = jnp.full((8, SLOTS), fault_count[0], jnp.int32).astype(F32)
    copies[0].wait()
    ordered = order_rows(restriction_here[...])
    for part in range(PARTS):
        copies[len(small) + part].wait()
        packed = state_here[:, part * width : (part + 1) * width].astype(BF16)
        make_traces(packed, ordered, table, part * TILES // PARTS, TILES // PARTS)
    for copy in copies[1 : len(small)]:
        copy.wait()
    pick_sent(table, send_here, plus_here, minus_here, sent, plus_out, minus_out, outgoing, out_sems)


def local_kernel(
    element_state, table, face_source, geometry, volume_ops, base, difference,
):
    state = element_state[...]
    packed = state.astype(BF16)
    operators = volume_ops[...].astype(F32)
    change = None
    for direction in range(3):
        operator = operators[direction * VALUES : (direction + 1) * VALUES].astype(BF16)
        term = jnp.dot(operator, packed, preferred_element_type=F32) * geometry[direction : direction + 1, :]
        change = term if change is None else change + term
    base[...] = state + TIME_STEP * change

    def body(face, carry):
        rows = pl.ds(pl.multiple_of(face * ROWS, ROWS), ROWS)
        for tile in range(TILES):
            columns = slice(tile * BLOCK, (tile + 1) * BLOCK)
            own = table[pl.ds(pl.multiple_of((face * TILES + tile) * ROWS, ROWS), ROWS), :].astype(F32)
            difference[rows, columns] = own - pick(table, face_source[pl.ds(face, 1), columns], 0, LOCAL)
        return carry

    lax.fori_loop(0, 4, body, 0)


def step_kernel(
    last, base, difference, received, partner, next_plus, next_constants, face_source, send_faces, plus_faces,
    minus_faces, own_plus, own_minus, fault_count, stress, state_variable, face_area, restriction, lift_operator,
    to_points, to_nodes, *rest,
):
    if last:
        state_out, slip_out, arrived, jump, masked, override, scaled, state_here, out_sems = rest
    else:
        state_out, sent, plus_out, minus_out, table, arrived, jump, masked, override, scaled, outgoing, out_sems = rest
    for block in range(REMOTE):
        arrived[block * ROWS : (block + 1) * ROWS, :] = jnp.concatenate(
            [received[2 * block], received[2 * block + 1]], axis=1
        )

    plus_side = jnp.concatenate([own_plus[...].astype(F32), next_plus[...].astype(F32)], axis=1)
    minus_side = jnp.concatenate([partner[...].astype(F32), own_minus[...].astype(F32)], axis=1)
    both_stress = jnp.concatenate([stress[...], next_constants[0:POINTS, :]], axis=1)
    both_state = jnp.concatenate([state_variable[...], next_constants[POINTS : 2 * POINTS, :]], axis=1)
    slip_rate = friction(plus_side - minus_side, both_stress, both_state, to_points[...], to_nodes[...], jump)
    slot = lax.broadcasted_iota(jnp.int32, (1, SLOTS), 1)
    own_live = slot < fault_count[0]
    next_live = slot.astype(F32) < next_constants[2 * POINTS : 2 * POINTS + 1, :]
    sign = jnp.concatenate([jnp.where(own_live, 1.0, 0.0), jnp.where(next_live, -1.0, 0.0)], axis=1)
    if last:
        slip_out[...] = jnp.where(own_live, slip_rate[:, :SLOTS], 0.0)

    row = lax.broadcasted_iota(jnp.int32, (ROWS, FAULTS), 0)
    jump[TRACE : TRACE + 2, :] = jnp.zeros((2, FAULTS), F32)
    values = jnp.where(row < TRACE, jump[...] * sign, jnp.where(row == TRACE, jnp.abs(sign), 0.0))
    coarse = values.astype(BF16).astype(F32)
    parts = jnp.concatenate([coarse, values - coarse], axis=0)
    faces = jnp.concatenate([plus_faces[...], minus_faces[...]], axis=1)
    high = jnp.broadcast_to(lax.shift_right_logical(faces, 8), parts.shape)
    for block in range(LOCAL):
        masked[block * 2 * ROWS : (block + 1) * 2 * ROWS, :] = jnp.where(high == block, parts, 0.0).astype(BF16)
    lanes = lax.broadcasted_iota(jnp.int32, (BLOCK, FAULTS), 0)
    selector = jnp.where(lanes == jnp.bitwise_and(faces, BLOCK - 1), 1.0, 0.0).astype(BF16)
    override[...] = lax.dot_general(masked[...], selector, (((1,), (1,)), ((), ())), preferred_element_type=F32)

    def body(face, carry):
        rows = pl.ds(pl.multiple_of(face * ROWS, ROWS), ROWS)
        for tile in range(TILES):
            columns = slice(tile * BLOCK, (tile + 1) * BLOCK)
            exterior = pick(arrived, face_source[pl.ds(face, 1), columns] - 4 * ELEMS, 0, REMOTE)
            start = (face * TILES + tile) * 2 * ROWS
            changed = (
                override[pl.ds(pl.multiple_of(start, ROWS), ROWS), :]
                + override[pl.ds(pl.multiple_of(start + ROWS, ROWS), ROWS), :]
            )
            plain = difference[rows, columns] - exterior
            face_jump = jnp.where(changed[TRACE : TRACE + 1] > 0.5, changed, plain)
            scaled[rows, columns] = (face_jump * face_area[pl.ds(face, 1), columns]).astype(BF16)
        return carry

    lax.fori_loop(0, 4, body, 0)

    lift = lax.dot_general(
        lift_operator[...], row_order(), (((1,), (1,)), ((), ())), preferred_element_type=F32
    ).astype(BF16)
    if not last:
        state = base[...] - TIME_STEP * jnp.dot(lift, scaled[...], preferred_element_type=F32)
        state_out[...] = state
        make_traces(state.astype(BF16), order_rows(restriction[...]), table, 0, TILES)
        pick_sent(table, send_faces, plus_faces, minus_faces, sent, plus_out, minus_out, outgoing, out_sems)
        return
    width = ELEMS // PARTS
    copies = []
    for part in range(PARTS):
        columns = slice(part * width, (part + 1) * width)
        lifted = jnp.dot(lift, scaled[:, columns], preferred_element_type=F32)
        state_here[:, columns] = base[:, columns] - TIME_STEP * lifted
        copies.append(pltpu.make_async_copy(state_here.at[:, columns], state_out.at[:, columns], out_sems.at[part]))
        copies[-1].start()
    for copy in copies:
        copy.wait()


VMEM = pl.BlockSpec(memory_space=pltpu.VMEM)
SMEM = pl.BlockSpec(memory_space=pltpu.SMEM)
ANY = pl.BlockSpec(memory_space=pl.ANY)


def call(kernel, name, args, specs, outs, out_specs, scratch, flops):
    return pl.pallas_call(
        kernel,
        out_shape=[jax.ShapeDtypeStruct(shape, dtype) for shape, dtype in outs],
        in_specs=specs,
        out_specs=out_specs,
        scratch_shapes=scratch,
        compiler_params=pltpu.CompilerParams(vmem_limit_bytes=VMEM_LIMIT),
        cost_estimate=pl.CostEstimate(flops=flops, bytes_accessed=4 * 2**20, transcendentals=0),
        name=name,
    )(*args)


def shards(
    element_state,
    face_source,
    send_faces,
    plus_faces,
    minus_faces,
    fault_count,
    normal_stress,
    state_variable,
    geometry,
    face_area,
    restriction,
    volume_ops,
    lift_operator,
    to_points,
    to_nodes,
):
    segments = lax.axis_size("seg")
    up = [(s, (s + 1) % segments) for s in range(segments)]
    down = [(s, (s - 1) % segments) for s in range(segments)]
    plus_faces = plus_faces.reshape(1, SLOTS)
    minus_faces = minus_faces.reshape(1, SLOTS)
    restriction = restriction.T
    side = ((ROWS, SLOTS), BF16)
    sent_shape = ((PEERS, ROWS, SLOTS), BF16)
    table_shape = ((LOCAL * ROWS, BLOCK), BF16)
    state_shape = (element_state.shape, F32)
    sent, constants, plus, minus, table = call(
        first_kernel,
        "first",
        (element_state, send_faces, plus_faces, minus_faces, normal_stress, state_variable, fault_count, restriction),
        [ANY] * 6 + [SMEM, ANY],
        [sent_shape, ((2 * POINTS + 8, SLOTS), F32), side, side, table_shape],
        [ANY] + [VMEM] * 4,
        [
            pltpu.VMEM(element_state.shape, F32),
            pltpu.VMEM(send_faces.shape, jnp.int32),
            pltpu.VMEM(plus_faces.shape, jnp.int32),
            pltpu.VMEM(minus_faces.shape, jnp.int32),
            pltpu.VMEM(restriction.shape, BF16),
            pltpu.VMEM(*sent_shape),
            pltpu.SemaphoreType.DMA((6 + PARTS,)),
            pltpu.SemaphoreType.DMA((PEERS // 8,)),
        ],
        2 * 10**9,
    )
    next_constants = lax.ppermute(constants, "seg", down)
    for step in range(STEPS):
        last = step == STEPS - 1
        received = lax.all_to_all(sent, "dom", 0, 0, tiled=True)
        partner = lax.ppermute(minus, "seg", up)
        next_plus = lax.ppermute(plus, "seg", down)
        base, difference = call(
            local_kernel,
            "local",
            (element_state, table, face_source, geometry, volume_ops),
            [VMEM] * 5,
            [state_shape, ((4 * ROWS, ELEMS), F32)],
            [VMEM] * 2,
            [],
            4 * 10**9,
        )
        args = (
            base, difference, received, partner, next_plus, next_constants, face_source, send_faces, plus_faces,
            minus_faces, plus, minus, fault_count, normal_stress, state_variable, face_area, restriction,
            lift_operator, to_points, to_nodes,
        )
        specs = [SMEM if arg is fault_count else VMEM for arg in args]
        scratch = [
            pltpu.VMEM((REMOTE * ROWS, BLOCK), BF16),
            pltpu.VMEM((ROWS, FAULTS), F32),
            pltpu.VMEM((LOCAL * 2 * ROWS, FAULTS), BF16),
            pltpu.VMEM((LOCAL * 2 * ROWS, BLOCK), F32),
            pltpu.VMEM((4 * ROWS, ELEMS), BF16),
        ]
        kernel = functools.partial(step_kernel, last)
        if last:
            scratch += [pltpu.VMEM(*state_shape), pltpu.SemaphoreType.DMA((PARTS,))]
            outs = [state_shape, (normal_stress.shape, F32)]
            return tuple(call(kernel, "last", args, specs, outs, [ANY, VMEM], scratch, 4 * 10**9))
        scratch += [pltpu.VMEM(*sent_shape), pltpu.SemaphoreType.DMA((PEERS // 8,))]
        outs = [state_shape, sent_shape, side, side, table_shape]
        element_state, sent, plus, minus, table = call(
            kernel, "step", args, specs, outs, [VMEM, ANY, VMEM, VMEM, VMEM], scratch, 4 * 10**9
        )


def solution(mesh):
    placed = (
        P(None, ("seg", "dom")),
        P(None, ("seg", "dom")),
        P(None, ("seg", "dom")),
        P(("seg", "dom")),
        P(("seg", "dom")),
        P(("seg", "dom")),
        P(None, ("seg", "dom")),
        P(None, ("seg", "dom")),
        P(None, ("seg", "dom")),
        P(None, ("seg", "dom")),
        P(),
        P(),
        P(),
        P(),
        P(),
    )
    return jax.shard_map(
        shards,
        mesh=mesh,
        in_specs=placed,
        out_specs=(P(None, ("seg", "dom")), P(None, ("seg", "dom"))),
        check_vma=False,
    )
```

```python
import functools

import jax
import jax.numpy as jnp
from jax import lax
from jax.experimental import pallas as pl
from jax.experimental.pallas import tpu as pltpu
from jax.sharding import PartitionSpec as P

STEPS = 2
NEWTON = 4
IMPEDANCE = 1.0
FRICTION_A = 0.2
REGULARIZE = 0.25
TIME_STEP = 0.25

F32 = jnp.float32
BF16 = jnp.bfloat16

VALUES = 180
TRACE = 30
ROWS = 32
ELEMS = 1536
PEERS = 32
SLOTS = 128
POINTS = 16
NODES = 10
BLOCK = 256
TILES = ELEMS // BLOCK
LOCAL = 4 * TILES
REMOTE = PEERS * SLOTS // BLOCK
FAULTS = 2 * SLOTS
PARTS = 3
EARLY = 2
VMEM_LIMIT = 32 * 2**20


def inverse_sinh(value):
    return jnp.log(value + jnp.sqrt(value * value + 1.0))


def row_order():
    row = lax.broadcasted_iota(jnp.int32, (4 * ROWS, 4 * TRACE), 0)
    column = lax.broadcasted_iota(jnp.int32, (4 * ROWS, 4 * TRACE), 1)
    face = lax.shift_right_logical(row, 5)
    value = jnp.bitwise_and(row, ROWS - 1)
    return jnp.where(column == 4 * value + face, 1.0, 0.0).astype(BF16)


def make_traces(packed, ordered, table, first, tiles):
    made = jnp.dot(ordered, packed, preferred_element_type=F32).astype(BF16)
    for face in range(4):
        for tile in range(tiles):
            start = (face * TILES + first + tile) * ROWS
            table[start : start + ROWS, :] = made[face * ROWS : (face + 1) * ROWS, tile * BLOCK : (tile + 1) * BLOCK]


def order_rows(order, restriction):
    return lax.dot_general(order, restriction, (((1,), (1,)), ((), ())), preferred_element_type=F32).astype(BF16)


def pick(table, index, first, blocks):
    width = index.shape[1]
    low = jnp.bitwise_and(index, BLOCK - 1)
    high = jnp.broadcast_to(lax.shift_right_arithmetic(index, 8), (8, width))
    lanes = lax.broadcasted_iota(jnp.int32, (BLOCK, width), 0)
    selector = jnp.where(lanes == low, 1.0, 0.0).astype(BF16)
    product = jnp.dot(table[first * ROWS : (first + blocks) * ROWS, :], selector, preferred_element_type=F32)
    product = product.reshape(blocks, ROWS // 8, 8, width)
    picked = jnp.zeros((ROWS // 8, 8, width), F32)
    for block in range(blocks):
        here = jnp.broadcast_to((high == first + block)[None], picked.shape)
        picked = jnp.where(here, product[block], picked)
    return picked.reshape(ROWS, width)


def pick_sent(table, send_faces, plus_faces, minus_faces, sent, sides_out, outgoing, sides, sems):
    index = jnp.concatenate([plus_faces[...], minus_faces[...]], axis=1)
    picked = pick(table, index, 0, LOCAL).astype(BF16)
    copies = []
    for i in range(2):
        sides[i] = picked[:, i * SLOTS : (i + 1) * SLOTS]
        copies.append(pltpu.make_async_copy(sides.at[i], sides_out[i], sems.at[PEERS // 8 + i]))
        copies[-1].start()

    def body(turn, carry):
        start = turn * 8
        faces = send_faces[pl.ds(start, 8), :]
        for pair in range(4):
            index = jnp.concatenate([faces[2 * pair : 2 * pair + 1], faces[2 * pair + 1 : 2 * pair + 2]], axis=1)
            picked = pick(table, index, 0, LOCAL).astype(BF16)
            outgoing[start + 2 * pair] = picked[:, :SLOTS]
            outgoing[start + 2 * pair + 1] = picked[:, SLOTS:]
        part = pl.ds(start, 8)
        pltpu.make_async_copy(outgoing.at[part], sent.at[part], sems.at[turn]).start()
        return carry

    for turn in range(PEERS // 8):
        body(turn, 0)
    for turn in range(PEERS // 8):
        part = slice(turn * 8, turn * 8 + 8)
        copies.append(pltpu.make_async_copy(outgoing.at[part], sent.at[part], sems.at[turn]))
    for copy in copies:
        copy.wait()


def friction(difference, stress, state, to_points, to_nodes, jump):
    weights = [jnp.broadcast_to(to_points[:, n : n + 1], stress.shape) for n in range(NODES)]
    at_points = []
    for component in range(3):
        total = weights[0] * difference[component * NODES : component * NODES + 1]
        for n in range(1, NODES):
            row = component * NODES + n
            total = total + weights[n] * difference[row : row + 1]
        at_points.append(total)
    magnitude = jnp.sqrt(at_points[1] * at_points[1] + at_points[2] * at_points[2] + REGULARIZE)
    rate_scale = 0.5 * jnp.exp(state)
    slip_rate = jnp.zeros_like(magnitude)
    for _ in range(NEWTON):
        scaled_rate = slip_rate * rate_scale
        residual_value = IMPEDANCE * (magnitude - slip_rate) - stress * FRICTION_A * inverse_sinh(scaled_rate)
        derivative = IMPEDANCE + stress * FRICTION_A * rate_scale / jnp.sqrt(1.0 + scaled_rate * scaled_rate)
        slip_rate = slip_rate + residual_value / derivative
    share = slip_rate / magnitude
    point_jump = [at_points[0], at_points[1] * share, at_points[2] * share]
    columns = [jnp.broadcast_to(to_nodes[:, q : q + 1], (NODES, stress.shape[1])) for q in range(POINTS)]
    for component in range(3):
        total = columns[0] * point_jump[component][0:1]
        for q in range(1, POINTS):
            total = total + columns[q] * point_jump[component][q : q + 1]
        jump[component * NODES : (component + 1) * NODES, :] = total
    return slip_rate


def order_kernel(order):
    order[...] = row_order()


def first_kernel(
    order, element_state, send_faces, plus_faces, minus_faces, stress, state_variable, fault_count, restriction,
    sent, constants, plus_out, minus_out, table, outgoing, sides, sems,
):
    make_traces(element_state[...].astype(BF16), order_rows(order[...], restriction[...]), table, 0, TILES)
    constants[0:POINTS, :] = stress[...]
    constants[POINTS : 2 * POINTS, :] = state_variable[...]
    constants[2 * POINTS :, :] = jnp.full((8, SLOTS), fault_count[0], jnp.int32).astype(F32)
    pick_sent(table, send_faces, plus_faces, minus_faces, sent, [plus_out, minus_out], outgoing, sides, sems)


def early_kernel(element_state, table, face_source, geometry, volume_ops, base, difference):
    state = element_state[...]
    packed = state.astype(BF16)
    operators = volume_ops[...].astype(F32).T
    change = None
    for direction in range(3):
        operator = operators[direction * VALUES : (direction + 1) * VALUES].astype(BF16)
        term = jnp.dot(operator, packed, preferred_element_type=F32) * geometry[direction : direction + 1, :]
        change = term if change is None else change + term
    base[...] = state + TIME_STEP * change

    def body(face, carry):
        rows = pl.ds(face * ROWS, ROWS)
        for tile in range(TILES):
            columns = slice(tile * BLOCK, (tile + 1) * BLOCK)
            own = table[pl.ds((face * TILES + tile) * ROWS, ROWS), :].astype(F32)
            difference[rows, columns] = own - pick(table, face_source[pl.ds(face, 1), columns], 0, LOCAL)
        return carry

    for face in range(EARLY):
        body(face, 0)


def step_kernel(
    last, order, base, difference, table_in, received, partner, next_plus, next_constants, face_source, send_faces, plus_faces,
    minus_faces, own_plus, own_minus, fault_count, stress, state_variable, face_area, restriction, lift_operator,
    to_points, to_nodes, *rest,
):
    if last:
        state_out, slip_out, table, jump, masked, override, scaled, state, out_sems = rest
    else:
        state_out, sent, plus_out, minus_out, table_out = rest[:5]
        table, jump, masked, override, scaled, outgoing, sides, own_sems = rest[5:]
        state = state_out
    table[0 : LOCAL * ROWS, :] = table_in[...]
    for block in range(REMOTE):
        table[(LOCAL + block) * ROWS : (LOCAL + block + 1) * ROWS, :] = jnp.concatenate(
            [received[2 * block], received[2 * block + 1]], axis=1
        )

    plus_side = jnp.concatenate([own_plus[...].astype(F32), next_plus[...].astype(F32)], axis=1)
    minus_side = jnp.concatenate([partner[...].astype(F32), own_minus[...].astype(F32)], axis=1)
    both_stress = jnp.concatenate([stress[...], next_constants[0:POINTS, :]], axis=1)
    both_state = jnp.concatenate([state_variable[...], next_constants[POINTS : 2 * POINTS, :]], axis=1)
    slip_rate = friction(plus_side - minus_side, both_stress, both_state, to_points[...], to_nodes[...], jump)
    slot = lax.broadcasted_iota(jnp.int32, (1, SLOTS), 1)
    own_live = slot < fault_count[0]
    next_live = slot.astype(F32) < next_constants[2 * POINTS : 2 * POINTS + 1, :]
    sign = jnp.concatenate([jnp.where(own_live, 1.0, 0.0), jnp.where(next_live, -1.0, 0.0)], axis=1)
    if last:
        slip_out[...] = jnp.where(own_live, slip_rate[:, :SLOTS], 0.0)

    row = lax.broadcasted_iota(jnp.int32, (ROWS, FAULTS), 0)
    jump[TRACE : TRACE + 2, :] = jnp.zeros((2, FAULTS), F32)
    values = jnp.where(row < TRACE, jump[...] * sign, jnp.where(row == TRACE, jnp.abs(sign), 0.0))
    coarse = values.astype(BF16).astype(F32)
    parts = jnp.concatenate([coarse, values - coarse], axis=0)
    faces = jnp.concatenate([plus_faces[...], minus_faces[...]], axis=1)
    high = jnp.broadcast_to(lax.shift_right_logical(faces, 8), parts.shape)
    for block in range(LOCAL):
        masked[block * 2 * ROWS : (block + 1) * 2 * ROWS, :] = jnp.where(high == block, parts, 0.0).astype(BF16)
    lanes = lax.broadcasted_iota(jnp.int32, (BLOCK, FAULTS), 0)
    selector = jnp.where(lanes == jnp.bitwise_and(faces, BLOCK - 1), 1.0, 0.0).astype(BF16)
    override[...] = lax.dot_general(masked[...], selector, (((1,), (1,)), ((), ())), preferred_element_type=F32)

    def body(early, face, carry):
        rows = pl.ds(face * ROWS, ROWS)
        for tile in range(TILES):
            columns = slice(tile * BLOCK, (tile + 1) * BLOCK)
            index = face_source[pl.ds(face, 1), columns]
            if early:
                plain = difference[rows, columns] - pick(table, index, LOCAL, REMOTE)
            else:
                own = table_in[pl.ds((face * TILES + tile) * ROWS, ROWS), :].astype(F32)
                plain = own - pick(table, index, 0, LOCAL + REMOTE)
            start = (face * TILES + tile) * 2 * ROWS
            changed = (
                override[pl.ds(start, ROWS), :]
                + override[pl.ds(start + ROWS, ROWS), :]
            )
            face_jump = jnp.where(changed[TRACE : TRACE + 1] > 0.5, changed, plain)
            scaled[rows, columns] = (face_jump * face_area[pl.ds(face, 1), columns]).astype(BF16)
        return carry

    for face in range(4):
        body(face < EARLY, face, 0)

    lift = lax.dot_general(
        lift_operator[...], order[...], (((1,), (1,)), ((), ())), preferred_element_type=F32
    ).astype(BF16)
    if not last:
        state[...] = base[...] - TIME_STEP * jnp.dot(lift, scaled[...], preferred_element_type=F32)
        make_traces(state[...].astype(BF16), order_rows(order[...], restriction[...]), table, 0, TILES)
        table_out[...] = table[0 : LOCAL * ROWS, :]
        pick_sent(table, send_faces, plus_faces, minus_faces, sent, [plus_out, minus_out], outgoing, sides, own_sems)
        return
    width = ELEMS // PARTS
    copies = []
    for part in range(PARTS):
        columns = slice(part * width, (part + 1) * width)
        lifted = jnp.dot(lift, scaled[:, columns], preferred_element_type=F32)
        state[:, columns] = base[:, columns] - TIME_STEP * lifted
        copies.append(pltpu.make_async_copy(state.at[:, columns], state_out.at[:, columns], out_sems.at[part]))
        copies[-1].start()
    for copy in copies:
        copy.wait()


VMEM = pl.BlockSpec(memory_space=pltpu.VMEM)
SMEM = pl.BlockSpec(memory_space=pltpu.SMEM)
HBM = pl.BlockSpec(memory_space=pltpu.HBM)


def call(kernel, name, args, specs, outs, out_specs, scratch, flops):
    return pl.pallas_call(
        kernel,
        out_shape=[jax.ShapeDtypeStruct(shape, dtype) for shape, dtype in outs],
        in_specs=specs,
        out_specs=out_specs,
        scratch_shapes=scratch,
        compiler_params=pltpu.CompilerParams(vmem_limit_bytes=VMEM_LIMIT),
        cost_estimate=pl.CostEstimate(flops=flops, bytes_accessed=4 * 2**20, transcendentals=0),
        name=name,
    )(*args)


def shards(
    element_state,
    face_source,
    send_faces,
    plus_faces,
    minus_faces,
    fault_count,
    normal_stress,
    state_variable,
    geometry,
    face_area,
    restriction,
    volume_ops,
    lift_operator,
    to_points,
    to_nodes,
):
    segments = lax.axis_size("seg")
    up = [(s, (s + 1) % segments) for s in range(segments)]
    down = [(s, (s - 1) % segments) for s in range(segments)]
    plus_faces = plus_faces.reshape(1, SLOTS)
    minus_faces = minus_faces.reshape(1, SLOTS)
    restriction = restriction.T
    volume_ops = volume_ops.T
    side = ((ROWS, SLOTS), BF16)
    sent_shape = ((PEERS, ROWS, SLOTS), BF16)
    table_shape = ((LOCAL * ROWS, BLOCK), BF16)
    state_shape = (element_state.shape, F32)
    (order,) = call(order_kernel, "order", (), [], [((4 * ROWS, 4 * TRACE), BF16)], [VMEM], [], 4 * 10**9)
    sent, constants, plus, minus, table = call(
        first_kernel,
        "first",
        (
            order, element_state, send_faces, plus_faces, minus_faces, normal_stress, state_variable, fault_count,
            restriction,
        ),
        [VMEM] * 7 + [SMEM, VMEM],
        [sent_shape, ((2 * POINTS + 8, SLOTS), F32), side, side, table_shape],
        [HBM, VMEM, HBM, HBM, VMEM],
        [
            pltpu.VMEM(*sent_shape),
            pltpu.VMEM((2, ROWS, SLOTS), BF16),
            pltpu.SemaphoreType.DMA((PEERS // 8 + 2,)),
        ],
        2 * 10**9,
    )
    next_constants = lax.ppermute(constants, "seg", down)
    for step in range(STEPS):
        last = step == STEPS - 1
        received = lax.all_to_all(sent, "dom", 0, 0, tiled=True)
        partner = lax.ppermute(minus, "seg", up)
        next_plus = lax.ppermute(plus, "seg", down)
        base, difference = call(
            early_kernel,
            "early",
            (element_state, table, face_source, geometry, volume_ops),
            [VMEM] * 5,
            [state_shape, ((EARLY * ROWS, ELEMS), F32)],
            [VMEM] * 2,
            [],
            2 * 10**9,
        )
        args = (
            order, base, difference, table, received, partner, next_plus, next_constants, face_source, send_faces, plus_faces,
            minus_faces, plus, minus, fault_count, normal_stress, state_variable, face_area, restriction,
            lift_operator, to_points, to_nodes,
        )
        specs = [SMEM if arg is fault_count else VMEM for arg in args]
        scratch = [
            pltpu.VMEM(((LOCAL + REMOTE) * ROWS, BLOCK), BF16),
            pltpu.VMEM((ROWS, FAULTS), F32),
            pltpu.VMEM((LOCAL * 2 * ROWS, FAULTS), BF16),
            pltpu.VMEM((LOCAL * 2 * ROWS, BLOCK), F32),
            pltpu.VMEM((4 * ROWS, ELEMS), BF16),
        ]
        kernel = functools.partial(step_kernel, last)
        if last:
            scratch += [pltpu.VMEM(*state_shape), pltpu.SemaphoreType.DMA((PARTS,))]
            outs = [state_shape, (normal_stress.shape, F32)]
            return tuple(call(kernel, "last", args, specs, outs, [HBM, VMEM], scratch, 4 * 10**9))
        scratch += [
            pltpu.VMEM(*sent_shape),
            pltpu.VMEM((2, ROWS, SLOTS), BF16),
            pltpu.SemaphoreType.DMA((PEERS // 8 + 2,)),
        ]
        outs = [state_shape, sent_shape, side, side, table_shape]
        element_state, sent, plus, minus, table = call(
            kernel, "step", args, specs, outs, [VMEM, HBM, HBM, HBM, VMEM], scratch, 4 * 10**9
        )


def solution(mesh):
    placed = (
        P(None, ("seg", "dom")),
        P(None, ("seg", "dom")),
        P(None, ("seg", "dom")),
        P(("seg", "dom")),
        P(("seg", "dom")),
        P(("seg", "dom")),
        P(None, ("seg", "dom")),
        P(None, ("seg", "dom")),
        P(None, ("seg", "dom")),
        P(None, ("seg", "dom")),
        P(),
        P(),
        P(),
        P(),
        P(),
    )
    return jax.shard_map(
        shards,
        mesh=mesh,
        in_specs=placed,
        out_specs=(P(None, ("seg", "dom")), P(None, ("seg", "dom"))),
        check_vma=False,
    )
```

```python
import functools

import jax
import jax.numpy as jnp
from jax import lax
from jax.experimental import pallas as pl
from jax.experimental.pallas import tpu as pltpu
from jax.sharding import PartitionSpec as P

STEPS = 2
NEWTON = 4
IMPEDANCE = 1.0
FRICTION_A = 0.2
REGULARIZE = 0.25
TIME_STEP = 0.25

F32 = jnp.float32
BF16 = jnp.bfloat16

VALUES = 180
TRACE = 30
ROWS = 32
ELEMS = 1536
PEERS = 32
SLOTS = 128
POINTS = 16
NODES = 10
BLOCK = 256
TILES = ELEMS // BLOCK
LOCAL = 4 * TILES
REMOTE = PEERS * SLOTS // BLOCK
FAULTS = 2 * SLOTS
PARTS = 3
VMEM_LIMIT = 32 * 2**20


def inverse_sinh(value):
    return jnp.log(value + jnp.sqrt(value * value + 1.0))


def row_order():
    row = lax.broadcasted_iota(jnp.int32, (4 * ROWS, 4 * TRACE), 0)
    column = lax.broadcasted_iota(jnp.int32, (4 * ROWS, 4 * TRACE), 1)
    face = lax.shift_right_logical(row, 5)
    value = jnp.bitwise_and(row, ROWS - 1)
    return jnp.where(column == 4 * value + face, 1.0, 0.0).astype(BF16)


def make_traces(packed, ordered, table, first, tiles):
    made = jnp.dot(ordered, packed, preferred_element_type=F32).astype(BF16)
    for face in range(4):
        for tile in range(tiles):
            start = (face * TILES + first + tile) * ROWS
            table[start : start + ROWS, :] = made[face * ROWS : (face + 1) * ROWS, tile * BLOCK : (tile + 1) * BLOCK]


def order_rows(order, restriction):
    return lax.dot_general(order, restriction, (((1,), (1,)), ((), ())), preferred_element_type=F32).astype(BF16)


def pick(table, index, first, blocks):
    width = index.shape[1]
    low = jnp.bitwise_and(index, BLOCK - 1)
    high = jnp.broadcast_to(lax.shift_right_arithmetic(index, 8), (8, width))
    lanes = lax.broadcasted_iota(jnp.int32, (BLOCK, width), 0)
    selector = jnp.where(lanes == low, 1.0, 0.0).astype(BF16)
    product = jnp.dot(table[first * ROWS : (first + blocks) * ROWS, :], selector, preferred_element_type=F32)
    product = product.reshape(blocks, ROWS // 8, 8, width)
    picked = jnp.zeros((ROWS // 8, 8, width), F32)
    for block in range(blocks):
        here = jnp.broadcast_to((high == first + block)[None], picked.shape)
        picked = jnp.where(here, product[block], picked)
    return picked.reshape(ROWS, width)


def pick_sent(table, send_faces, plus_faces, minus_faces, sent, plus_out, minus_out, outgoing, sems):
    index = jnp.concatenate([plus_faces[...], minus_faces[...]], axis=1)
    picked = pick(table, index, 0, LOCAL).astype(BF16)
    plus_out[...] = picked[:, :SLOTS]
    minus_out[...] = picked[:, SLOTS:]
    copies = []
    for turn in range(PEERS // 8):
        start = turn * 8
        for pair in range(start, start + 8, 2):
            index = jnp.concatenate([send_faces[pair : pair + 1, :], send_faces[pair + 1 : pair + 2, :]], axis=1)
            picked = pick(table, index, 0, LOCAL).astype(BF16)
            outgoing[pair] = picked[:, :SLOTS]
            outgoing[pair + 1] = picked[:, SLOTS:]
        part = slice(start, start + 8)
        copies.append(pltpu.make_async_copy(outgoing.at[part], sent.at[part], sems.at[turn]))
        copies[-1].start()
    for copy in copies:
        copy.wait()


def friction(difference, stress, state, to_points, to_nodes, jump):
    weights = [jnp.broadcast_to(to_points[:, n : n + 1], stress.shape) for n in range(NODES)]
    at_points = []
    for component in range(3):
        total = weights[0] * difference[component * NODES : component * NODES + 1]
        for n in range(1, NODES):
            row = component * NODES + n
            total = total + weights[n] * difference[row : row + 1]
        at_points.append(total)
    magnitude = jnp.sqrt(at_points[1] * at_points[1] + at_points[2] * at_points[2] + REGULARIZE)
    rate_scale = 0.5 * jnp.exp(state)
    slip_rate = jnp.zeros_like(magnitude)
    for _ in range(NEWTON):
        scaled_rate = slip_rate * rate_scale
        residual_value = IMPEDANCE * (magnitude - slip_rate) - stress * FRICTION_A * inverse_sinh(scaled_rate)
        derivative = IMPEDANCE + stress * FRICTION_A * rate_scale / jnp.sqrt(1.0 + scaled_rate * scaled_rate)
        slip_rate = slip_rate + residual_value / derivative
    share = slip_rate / magnitude
    point_jump = [at_points[0], at_points[1] * share, at_points[2] * share]
    columns = [jnp.broadcast_to(to_nodes[:, q : q + 1], (NODES, stress.shape[1])) for q in range(POINTS)]
    for component in range(3):
        total = columns[0] * point_jump[component][0:1]
        for q in range(1, POINTS):
            total = total + columns[q] * point_jump[component][q : q + 1]
        jump[component * NODES : (component + 1) * NODES, :] = total
    return slip_rate


def order_kernel(order):
    order[...] = row_order()


def first_kernel(
    order, element_state, send_faces, plus_faces, minus_faces, stress, state_variable, fault_count, restriction,
    sent, constants, plus_out, minus_out, table, outgoing, sems,
):
    make_traces(element_state[...].astype(BF16), order_rows(order[...], restriction[...]), table, 0, TILES)
    constants[0:POINTS, :] = stress[...]
    constants[POINTS : 2 * POINTS, :] = state_variable[...]
    constants[2 * POINTS :, :] = jnp.full((8, SLOTS), fault_count[0], jnp.int32).astype(F32)
    pick_sent(table, send_faces, plus_faces, minus_faces, sent, plus_out, minus_out, outgoing, sems)


def early_kernel(
    element_state, table, face_source, geometry, volume_ops, base_out, difference, state, base, sems,
):
    state_copy = pltpu.make_async_copy(element_state, state, sems.at[0])
    state_copy.start()

    def take(face):
        rows = slice(face * ROWS, (face + 1) * ROWS)
        for tile in range(TILES):
            columns = slice(tile * BLOCK, (tile + 1) * BLOCK)
            start = (face * TILES + tile) * ROWS
            own = table[start : start + ROWS, :].astype(F32)
            difference[rows, columns] = own - pick(table, face_source[face : face + 1, columns], 0, LOCAL)

    take(0)
    take(1)
    state_copy.wait()
    packed = state[...].astype(BF16)
    operators = volume_ops[...].astype(F32).T
    change = None
    for direction in range(3):
        operator = operators[direction * VALUES : (direction + 1) * VALUES].astype(BF16)
        term = jnp.dot(operator, packed, preferred_element_type=F32) * geometry[direction : direction + 1, :]
        change = term if change is None else change + term
    base[...] = state[...] + TIME_STEP * change
    base_copy = pltpu.make_async_copy(base, base_out, sems.at[1])
    base_copy.start()
    take(2)
    take(3)
    base_copy.wait()


def step_kernel(
    last, order, base_in, difference, received, partner, next_plus, next_constants, face_source, send_faces, plus_faces,
    minus_faces, own_plus, own_minus, fault_count, stress, state_variable, face_area, restriction, lift_operator,
    to_points, to_nodes, *rest,
):
    if last:
        state_out, slip_out, arrived, jump, masked, override, scaled, base, state, sems = rest
    else:
        state_out, sent, plus_out, minus_out, table = rest[:5]
        arrived, jump, masked, override, scaled, base, state, sems, outgoing, own_sems = rest[5:]
    base_copy = pltpu.make_async_copy(base_in, base, sems.at[PARTS])
    base_copy.start()
    for block in range(REMOTE):
        arrived[block * ROWS : (block + 1) * ROWS, :] = jnp.concatenate(
            [received[2 * block], received[2 * block + 1]], axis=1
        )

    plus_side = jnp.concatenate([own_plus[...].astype(F32), next_plus[...].astype(F32)], axis=1)
    minus_side = jnp.concatenate([partner[...].astype(F32), own_minus[...].astype(F32)], axis=1)
    both_stress = jnp.concatenate([stress[...], next_constants[0:POINTS, :]], axis=1)
    both_state = jnp.concatenate([state_variable[...], next_constants[POINTS : 2 * POINTS, :]], axis=1)
    slip_rate = friction(plus_side - minus_side, both_stress, both_state, to_points[...], to_nodes[...], jump)
    slot = lax.broadcasted_iota(jnp.int32, (1, SLOTS), 1)
    own_live = slot < fault_count[0]
    next_live = slot.astype(F32) < next_constants[2 * POINTS : 2 * POINTS + 1, :]
    sign = jnp.concatenate([jnp.where(own_live, 1.0, 0.0), jnp.where(next_live, -1.0, 0.0)], axis=1)
    if last:
        slip_out[...] = jnp.where(own_live, slip_rate[:, :SLOTS], 0.0)

    row = lax.broadcasted_iota(jnp.int32, (ROWS, FAULTS), 0)
    jump[TRACE : TRACE + 2, :] = jnp.zeros((2, FAULTS), F32)
    values = jnp.where(row < TRACE, jump[...] * sign, jnp.where(row == TRACE, jnp.abs(sign), 0.0))
    coarse = values.astype(BF16).astype(F32)
    parts = jnp.concatenate([coarse, values - coarse], axis=0)
    faces = jnp.concatenate([plus_faces[...], minus_faces[...]], axis=1)
    high = jnp.broadcast_to(lax.shift_right_logical(faces, 8), parts.shape)
    for block in range(LOCAL):
        masked[block * 2 * ROWS : (block + 1) * 2 * ROWS, :] = jnp.where(high == block, parts, 0.0).astype(BF16)
    lanes = lax.broadcasted_iota(jnp.int32, (BLOCK, FAULTS), 0)
    selector = jnp.where(lanes == jnp.bitwise_and(faces, BLOCK - 1), 1.0, 0.0).astype(BF16)
    override[...] = lax.dot_general(masked[...], selector, (((1,), (1,)), ((), ())), preferred_element_type=F32)

    for face in range(4):
        rows = slice(face * ROWS, (face + 1) * ROWS)
        for tile in range(TILES):
            columns = slice(tile * BLOCK, (tile + 1) * BLOCK)
            index = face_source[face : face + 1, columns] - 4 * ELEMS
            plain = difference[rows, columns] - pick(arrived, index, 0, REMOTE)
            start = (face * TILES + tile) * 2 * ROWS
            changed = override[start : start + ROWS, :] + override[start + ROWS : start + 2 * ROWS, :]
            face_jump = jnp.where(changed[TRACE : TRACE + 1] > 0.5, changed, plain)
            scaled[rows, columns] = (face_jump * face_area[face : face + 1, columns]).astype(BF16)

    lift = lax.dot_general(
        lift_operator[...], order[...], (((1,), (1,)), ((), ())), preferred_element_type=F32
    ).astype(BF16)
    base_copy.wait()
    width = ELEMS // PARTS
    copies = []
    for part in range(PARTS):
        columns = slice(part * width, (part + 1) * width)
        lifted = jnp.dot(lift, scaled[:, columns], preferred_element_type=F32)
        state[:, columns] = base[:, columns] - TIME_STEP * lifted
        copies.append(pltpu.make_async_copy(state.at[:, columns], state_out.at[:, columns], sems.at[part]))
        copies[-1].start()
    if not last:
        make_traces(state[...].astype(BF16), order_rows(order[...], restriction[...]), table, 0, TILES)
        pick_sent(table, send_faces, plus_faces, minus_faces, sent, plus_out, minus_out, outgoing, own_sems)
    for copy in copies:
        copy.wait()


VMEM = pl.BlockSpec(memory_space=pltpu.VMEM)
SMEM = pl.BlockSpec(memory_space=pltpu.SMEM)
HBM = pl.BlockSpec(memory_space=pltpu.HBM)


def call(kernel, name, args, specs, outs, out_specs, scratch, flops):
    return pl.pallas_call(
        kernel,
        out_shape=[
            pltpu.HBM(shape, dtype) if spec is HBM else jax.ShapeDtypeStruct(shape, dtype)
            for (shape, dtype), spec in zip(outs, out_specs, strict=True)
        ],
        in_specs=specs,
        out_specs=out_specs,
        scratch_shapes=scratch,
        compiler_params=pltpu.CompilerParams(vmem_limit_bytes=VMEM_LIMIT),
        cost_estimate=pl.CostEstimate(flops=flops, bytes_accessed=4 * 2**20, transcendentals=0),
        name=name,
    )(*[pltpu.with_memory_space_constraint(a, pltpu.HBM) if s is HBM else a for a, s in zip(args, specs, strict=True)])


def shards(
    element_state,
    face_source,
    send_faces,
    plus_faces,
    minus_faces,
    fault_count,
    normal_stress,
    state_variable,
    geometry,
    face_area,
    restriction,
    volume_ops,
    lift_operator,
    to_points,
    to_nodes,
):
    segments = lax.axis_size("seg")
    up = [(s, (s + 1) % segments) for s in range(segments)]
    down = [(s, (s - 1) % segments) for s in range(segments)]
    plus_faces = plus_faces.reshape(1, SLOTS)
    minus_faces = minus_faces.reshape(1, SLOTS)
    restriction = restriction.T
    volume_ops = volume_ops.T
    side = ((ROWS, SLOTS), BF16)
    sent_shape = ((PEERS, ROWS, SLOTS), BF16)
    table_shape = ((LOCAL * ROWS, BLOCK), BF16)
    state_shape = (element_state.shape, F32)
    (order,) = call(order_kernel, "order", (), [], [((4 * ROWS, 4 * TRACE), BF16)], [VMEM], [], 4 * 10**9)
    sent, constants, plus, minus, table = call(
        first_kernel,
        "first",
        (
            order, element_state, send_faces, plus_faces, minus_faces, normal_stress, state_variable, fault_count,
            restriction,
        ),
        [VMEM] * 7 + [SMEM, VMEM],
        [sent_shape, ((2 * POINTS + 8, SLOTS), F32), side, side, table_shape],
        [HBM, VMEM, VMEM, VMEM, VMEM],
        [
            pltpu.VMEM(*sent_shape),
            pltpu.SemaphoreType.DMA((PEERS // 8,)),
        ],
        2 * 10**9,
    )
    next_constants = lax.ppermute(constants, "seg", down)
    for step in range(STEPS):
        last = step == STEPS - 1
        received = lax.all_to_all(sent, "dom", 0, 0, tiled=True)
        partner = lax.ppermute(minus, "seg", up)
        next_plus = lax.ppermute(plus, "seg", down)
        base, difference = call(
            early_kernel,
            "early",
            (element_state, table, face_source, geometry, volume_ops),
            [HBM] + [VMEM] * 4,
            [state_shape, ((4 * ROWS, ELEMS), F32)],
            [HBM, VMEM],
            [pltpu.VMEM(*state_shape), pltpu.VMEM(*state_shape), pltpu.SemaphoreType.DMA((2,))],
            2 * 10**9,
        )
        args = (
            order, base, difference, received, partner, next_plus, next_constants, face_source, send_faces, plus_faces,
            minus_faces, plus, minus, fault_count, normal_stress, state_variable, face_area, restriction,
            lift_operator, to_points, to_nodes,
        )
        specs = [HBM if arg is base else SMEM if arg is fault_count else VMEM for arg in args]
        scratch = [
            pltpu.VMEM((REMOTE * ROWS, BLOCK), BF16),
            pltpu.VMEM((ROWS, FAULTS), F32),
            pltpu.VMEM((LOCAL * 2 * ROWS, FAULTS), BF16),
            pltpu.VMEM((LOCAL * 2 * ROWS, BLOCK), F32),
            pltpu.VMEM((4 * ROWS, ELEMS), BF16),
            pltpu.VMEM(*state_shape),
            pltpu.VMEM(*state_shape),
            pltpu.SemaphoreType.DMA((PARTS + 1,)),
        ]
        kernel = functools.partial(step_kernel, last)
        if last:
            outs = [state_shape, (normal_stress.shape, F32)]
            return tuple(call(kernel, "last", args, specs, outs, [HBM, VMEM], scratch, 4 * 10**9))
        scratch += [
            pltpu.VMEM(*sent_shape),
            pltpu.SemaphoreType.DMA((PEERS // 8,)),
        ]
        outs = [state_shape, sent_shape, side, side, table_shape]
        element_state, sent, plus, minus, table = call(
            kernel, "step", args, specs, outs, [HBM, HBM, VMEM, VMEM, VMEM], scratch, 4 * 10**9
        )


def solution(mesh):
    placed = (
        P(None, ("seg", "dom")),
        P(None, ("seg", "dom")),
        P(None, ("seg", "dom")),
        P(("seg", "dom")),
        P(("seg", "dom")),
        P(("seg", "dom")),
        P(None, ("seg", "dom")),
        P(None, ("seg", "dom")),
        P(None, ("seg", "dom")),
        P(None, ("seg", "dom")),
        P(),
        P(),
        P(),
        P(),
        P(),
    )
    return jax.shard_map(
        shards,
        mesh=mesh,
        in_specs=placed,
        out_specs=(P(None, ("seg", "dom")), P(None, ("seg", "dom"))),
        check_vma=False,
    )
```

```python
import functools

import jax
import jax.numpy as jnp
from jax import lax
from jax.experimental import pallas as pl
from jax.experimental.pallas import tpu as pltpu
from jax.sharding import PartitionSpec as P

STEPS = 2
NEWTON = 4
IMPEDANCE = 1.0
FRICTION_A = 0.2
REGULARIZE = 0.25
TIME_STEP = 0.25

F32 = jnp.float32
BF16 = jnp.bfloat16

VALUES = 180
TRACE = 30
ROWS = 32
ELEMS = 1536
PEERS = 32
SLOTS = 128
POINTS = 16
NODES = 10
BLOCK = 256
TILES = ELEMS // BLOCK
LOCAL = 4 * TILES
REMOTE = PEERS * SLOTS // BLOCK
FAULTS = 2 * SLOTS
PARTS = 6
SEND_CHUNK = 24
REMOTE_CHUNK = 8
LOCAL_CHUNK = 24
VMEM_LIMIT = 32 * 2**20


def inverse_sinh(value):
    return jnp.log(value + jnp.sqrt(value * value + 1.0))


def row_order():
    row = lax.broadcasted_iota(jnp.int32, (4 * ROWS, 4 * TRACE), 0)
    column = lax.broadcasted_iota(jnp.int32, (4 * ROWS, 4 * TRACE), 1)
    face = lax.shift_right_logical(row, 5)
    value = jnp.bitwise_and(row, ROWS - 1)
    return jnp.where(column == 4 * value + face, 1.0, 0.0).astype(BF16)


def make_traces(packed, ordered, table, first, tiles):
    made = jnp.dot(ordered, packed, preferred_element_type=F32).astype(BF16)
    for face in range(4):
        for tile in range(tiles):
            start = (face * TILES + first + tile) * ROWS
            table[start : start + ROWS, :] = made[face * ROWS : (face + 1) * ROWS, tile * BLOCK : (tile + 1) * BLOCK]


def order_rows(order, restriction):
    return lax.dot_general(order, restriction, (((1,), (1,)), ((), ())), preferred_element_type=F32).astype(BF16)


def pick(table, index, first, blocks, chunk):
    width = index.shape[1]
    low = jnp.bitwise_and(index, BLOCK - 1)
    high = jnp.broadcast_to(lax.shift_right_arithmetic(index, 8), (8, width))
    lanes = lax.broadcasted_iota(jnp.int32, (BLOCK, width), 0)
    selector = jnp.where(lanes == low, 1.0, 0.0).astype(BF16)
    picked = jnp.zeros((ROWS // 8, 8, width), F32)
    for part in range(0, blocks, chunk):
        start = (first + part) * ROWS
        product = jnp.dot(table[start : start + chunk * ROWS, :], selector, preferred_element_type=F32)
        product = product.reshape(chunk, ROWS // 8, 8, width)
        for block in range(chunk):
            here = jnp.broadcast_to((high == first + part + block)[None], picked.shape)
            picked = jnp.where(here, product[block], picked)
    return picked.reshape(ROWS, width)


def pick_sent(table, send_faces, plus_faces, minus_faces, sent, plus_out, minus_out):
    index = jnp.concatenate([plus_faces[...], minus_faces[...]], axis=1)
    picked = pick(table, index, 0, LOCAL, SEND_CHUNK).astype(BF16)
    plus_out[...] = picked[:, :SLOTS]
    minus_out[...] = picked[:, SLOTS:]
    for pair in range(0, PEERS, 2):
        index = jnp.concatenate([send_faces[pair : pair + 1, :], send_faces[pair + 1 : pair + 2, :]], axis=1)
        picked = pick(table, index, 0, LOCAL, SEND_CHUNK).astype(BF16)
        sent[pair] = picked[:, :SLOTS]
        sent[pair + 1] = picked[:, SLOTS:]


def friction(difference, stress, state, to_points, to_nodes, jump):
    weights = [jnp.broadcast_to(to_points[:, n : n + 1], stress.shape) for n in range(NODES)]
    at_points = []
    for component in range(3):
        total = weights[0] * difference[component * NODES : component * NODES + 1]
        for n in range(1, NODES):
            row = component * NODES + n
            total = total + weights[n] * difference[row : row + 1]
        at_points.append(total)
    magnitude = jnp.sqrt(at_points[1] * at_points[1] + at_points[2] * at_points[2] + REGULARIZE)
    rate_scale = 0.5 * jnp.exp(state)
    slip_rate = jnp.zeros_like(magnitude)
    for _ in range(NEWTON):
        scaled_rate = slip_rate * rate_scale
        residual_value = IMPEDANCE * (magnitude - slip_rate) - stress * FRICTION_A * inverse_sinh(scaled_rate)
        derivative = IMPEDANCE + stress * FRICTION_A * rate_scale / jnp.sqrt(1.0 + scaled_rate * scaled_rate)
        slip_rate = slip_rate + residual_value / derivative
    share = slip_rate / magnitude
    point_jump = [at_points[0], at_points[1] * share, at_points[2] * share]
    columns = [jnp.broadcast_to(to_nodes[:, q : q + 1], (NODES, stress.shape[1])) for q in range(POINTS)]
    for component in range(3):
        total = columns[0] * point_jump[component][0:1]
        for q in range(1, POINTS):
            total = total + columns[q] * point_jump[component][q : q + 1]
        jump[component * NODES : (component + 1) * NODES, :] = total
    return slip_rate


def order_kernel(order):
    order[...] = row_order()


def first_kernel(
    order, element_state, send_faces, plus_faces, minus_faces, stress, state_variable, fault_count, restriction,
    sent, constants, plus_out, minus_out, table,
):
    make_traces(element_state[...].astype(BF16), order_rows(order[...], restriction[...]), table, 0, TILES)
    constants[0:POINTS, :] = stress[...]
    constants[POINTS : 2 * POINTS, :] = state_variable[...]
    constants[2 * POINTS :, :] = jnp.full((8, SLOTS), fault_count[0], jnp.int32).astype(F32)
    pick_sent(table, send_faces, plus_faces, minus_faces, sent, plus_out, minus_out)


def early_kernel(
    element_state, table, face_source, geometry, volume_ops, base_out, difference, state, base, sems,
):
    state_copy = pltpu.make_async_copy(element_state, state, sems.at[0])
    state_copy.start()

    def take(face):
        rows = slice(face * ROWS, (face + 1) * ROWS)
        for tile in range(TILES):
            columns = slice(tile * BLOCK, (tile + 1) * BLOCK)
            start = (face * TILES + tile) * ROWS
            own = table[start : start + ROWS, :].astype(F32)
            difference[rows, columns] = own - pick(table, face_source[face : face + 1, columns], 0, LOCAL, LOCAL_CHUNK)

    take(0)
    take(1)
    state_copy.wait()
    packed = state[...].astype(BF16)
    operators = volume_ops[...].astype(F32).T
    change = None
    for direction in range(3):
        operator = operators[direction * VALUES : (direction + 1) * VALUES].astype(BF16)
        term = jnp.dot(operator, packed, preferred_element_type=F32) * geometry[direction : direction + 1, :]
        change = term if change is None else change + term
    base[...] = state[...] + TIME_STEP * change
    base_copy = pltpu.make_async_copy(base, base_out, sems.at[1])
    base_copy.start()
    take(2)
    take(3)
    base_copy.wait()


def fault_kernel(
    difference, partner, next_plus, next_constants, face_source, plus_faces, minus_faces, own_plus, own_minus,
    fault_count, stress, state_variable, to_points, to_nodes, plain, index_out, slip_out, jump, masked,
):
    plus_side = jnp.concatenate([own_plus[...].astype(F32), next_plus[...].astype(F32)], axis=1)
    minus_side = jnp.concatenate([partner[...].astype(F32), own_minus[...].astype(F32)], axis=1)
    both_stress = jnp.concatenate([stress[...], next_constants[0:POINTS, :]], axis=1)
    both_state = jnp.concatenate([state_variable[...], next_constants[POINTS : 2 * POINTS, :]], axis=1)
    slip_rate = friction(plus_side - minus_side, both_stress, both_state, to_points[...], to_nodes[...], jump)
    slot = lax.broadcasted_iota(jnp.int32, (1, SLOTS), 1)
    own_live = slot < fault_count[0]
    next_live = slot.astype(F32) < next_constants[2 * POINTS : 2 * POINTS + 1, :]
    sign = jnp.concatenate([jnp.where(own_live, 1.0, 0.0), jnp.where(next_live, -1.0, 0.0)], axis=1)
    slip_out[...] = jnp.where(own_live, slip_rate[:, :SLOTS], 0.0)

    row = lax.broadcasted_iota(jnp.int32, (ROWS, FAULTS), 0)
    jump[TRACE : TRACE + 2, :] = jnp.zeros((2, FAULTS), F32)
    values = jnp.where(row < TRACE, jump[...] * sign, jnp.where(row == TRACE, jnp.abs(sign), 0.0))
    coarse = values.astype(BF16).astype(F32)
    parts = jnp.concatenate([coarse, values - coarse], axis=0)
    faces = jnp.concatenate([plus_faces[...], minus_faces[...]], axis=1)
    high = jnp.broadcast_to(lax.shift_right_logical(faces, 8), parts.shape)
    for block in range(LOCAL):
        masked[block * 2 * ROWS : (block + 1) * 2 * ROWS, :] = jnp.where(high == block, parts, 0.0).astype(BF16)
    lanes = lax.broadcasted_iota(jnp.int32, (BLOCK, FAULTS), 0)
    selector = jnp.where(lanes == jnp.bitwise_and(faces, BLOCK - 1), 1.0, 0.0).astype(BF16)
    changed = lax.dot_general(masked[...], selector, (((1,), (1,)), ((), ())), preferred_element_type=F32)
    for face in range(4):
        rows = slice(face * ROWS, (face + 1) * ROWS)
        for tile in range(TILES):
            columns = slice(tile * BLOCK, (tile + 1) * BLOCK)
            start = (face * TILES + tile) * 2 * ROWS
            value = changed[start : start + ROWS, :] + changed[start + ROWS : start + 2 * ROWS, :]
            here = value[TRACE : TRACE + 1] > 0.5
            plain[rows, columns] = jnp.where(here, value, difference[rows, columns])
            index_out[face : face + 1, columns] = jnp.where(
                here, -1, face_source[face : face + 1, columns] - 4 * ELEMS
            )


def step_kernel(
    last, order, base_in, plain, received, index, face_area, restriction, lift_operator, send_faces, plus_faces,
    minus_faces, *rest,
):
    if last:
        state_out, arrived, scaled, base, state, sems = rest
    else:
        state_out, sent, plus_out, minus_out, table, arrived, scaled, base, state, sems = rest
    base_copy = pltpu.make_async_copy(base_in, base, sems.at[PARTS])
    base_copy.start()
    for block in range(REMOTE):
        arrived[block * ROWS : (block + 1) * ROWS, :] = jnp.concatenate(
            [received[2 * block], received[2 * block + 1]], axis=1
        )
    for face in range(4):
        rows = slice(face * ROWS, (face + 1) * ROWS)
        for tile in range(TILES):
            columns = slice(tile * BLOCK, (tile + 1) * BLOCK)
            face_jump = plain[rows, columns] - pick(arrived, index[face : face + 1, columns], 0, REMOTE, REMOTE_CHUNK)
            scaled[rows, columns] = (face_jump * face_area[face : face + 1, columns]).astype(BF16)
    lift = lax.dot_general(
        lift_operator[...], order[...], (((1,), (1,)), ((), ())), preferred_element_type=F32
    ).astype(BF16)
    base_copy.wait()
    width = ELEMS // PARTS
    copies = []
    for part in range(PARTS):
        columns = slice(part * width, (part + 1) * width)
        lifted = jnp.dot(lift, scaled[:, columns], preferred_element_type=F32)
        state[:, columns] = base[:, columns] - TIME_STEP * lifted
        copies.append(pltpu.make_async_copy(state.at[:, columns], state_out.at[:, columns], sems.at[part]))
        copies[-1].start()
    if not last:
        make_traces(state[...].astype(BF16), order_rows(order[...], restriction[...]), table, 0, TILES)
        pick_sent(table, send_faces, plus_faces, minus_faces, sent, plus_out, minus_out)
    for copy in copies:
        copy.wait()


VMEM = pl.BlockSpec(memory_space=pltpu.VMEM)
SMEM = pl.BlockSpec(memory_space=pltpu.SMEM)
HBM = pl.BlockSpec(memory_space=pltpu.HBM)


def call(kernel, name, args, specs, outs, out_specs, scratch, flops):
    return pl.pallas_call(
        kernel,
        out_shape=[
            pltpu.HBM(shape, dtype) if spec is HBM else jax.ShapeDtypeStruct(shape, dtype)
            for (shape, dtype), spec in zip(outs, out_specs, strict=True)
        ],
        in_specs=specs,
        out_specs=out_specs,
        scratch_shapes=scratch,
        compiler_params=pltpu.CompilerParams(vmem_limit_bytes=VMEM_LIMIT),
        cost_estimate=pl.CostEstimate(flops=flops, bytes_accessed=4 * 2**20, transcendentals=0),
        name=name,
    )(*[pltpu.with_memory_space_constraint(a, pltpu.HBM) if s is HBM else a for a, s in zip(args, specs, strict=True)])


def shards(
    element_state,
    face_source,
    send_faces,
    plus_faces,
    minus_faces,
    fault_count,
    normal_stress,
    state_variable,
    geometry,
    face_area,
    restriction,
    volume_ops,
    lift_operator,
    to_points,
    to_nodes,
):
    segments = lax.axis_size("seg")
    up = [(s, (s + 1) % segments) for s in range(segments)]
    down = [(s, (s - 1) % segments) for s in range(segments)]
    plus_faces = plus_faces.reshape(1, SLOTS)
    minus_faces = minus_faces.reshape(1, SLOTS)
    restriction = restriction.T
    volume_ops = volume_ops.T
    side = ((ROWS, SLOTS), BF16)
    sent_shape = ((PEERS, ROWS, SLOTS), BF16)
    table_shape = ((LOCAL * ROWS, BLOCK), BF16)
    state_shape = (element_state.shape, F32)
    (order,) = call(order_kernel, "order", (), [], [((4 * ROWS, 4 * TRACE), BF16)], [VMEM], [], 4 * 10**9)
    sent, constants, plus, minus, table = call(
        first_kernel,
        "first",
        (
            order, element_state, send_faces, plus_faces, minus_faces, normal_stress, state_variable, fault_count,
            restriction,
        ),
        [VMEM] * 7 + [SMEM, VMEM],
        [sent_shape, ((2 * POINTS + 8, SLOTS), F32), side, side, table_shape],
        [VMEM] * 5,
        [],
        2 * 10**9,
    )
    next_constants = lax.ppermute(constants, "seg", down)
    for step in range(STEPS):
        last = step == STEPS - 1
        received = lax.all_to_all(sent, "dom", 0, 0, tiled=True)
        partner = lax.ppermute(minus, "seg", up)
        next_plus = lax.ppermute(plus, "seg", down)
        base, difference = call(
            early_kernel,
            "early",
            (element_state, table, face_source, geometry, volume_ops),
            [HBM] + [VMEM] * 4,
            [state_shape, ((4 * ROWS, ELEMS), F32)],
            [HBM, VMEM],
            [pltpu.VMEM(*state_shape), pltpu.VMEM(*state_shape), pltpu.SemaphoreType.DMA((2,))],
            2 * 10**9,
        )
        plain, index, slip = call(
            fault_kernel,
            "fault",
            (
                difference, partner, next_plus, next_constants, face_source, plus_faces, minus_faces, plus, minus,
                fault_count, normal_stress, state_variable, to_points, to_nodes,
            ),
            [VMEM] * 9 + [SMEM] + [VMEM] * 4,
            [((4 * ROWS, ELEMS), F32), (face_source.shape, jnp.int32), (normal_stress.shape, F32)],
            [VMEM] * 3,
            [pltpu.VMEM((ROWS, FAULTS), F32), pltpu.VMEM((LOCAL * 2 * ROWS, FAULTS), BF16)],
            10**9,
        )
        args = (
            order, base, plain, received, index, face_area, restriction, lift_operator, send_faces, plus_faces,
            minus_faces,
        )
        specs = [VMEM, HBM] + [VMEM] * 9
        scratch = [
            pltpu.VMEM((REMOTE * ROWS, BLOCK), BF16),
            pltpu.VMEM((4 * ROWS, ELEMS), BF16),
            pltpu.VMEM(*state_shape),
            pltpu.VMEM(*state_shape),
            pltpu.SemaphoreType.DMA((PARTS + 1,)),
        ]
        kernel = functools.partial(step_kernel, last)
        if last:
            (element_state,) = call(kernel, "last", args, specs, [state_shape], [HBM], scratch, 4 * 10**9)
            return element_state, slip
        outs = [state_shape, sent_shape, side, side, table_shape]
        element_state, sent, plus, minus, table = call(
            kernel, "step", args, specs, outs, [HBM, VMEM, VMEM, VMEM, VMEM], scratch, 4 * 10**9
        )


def solution(mesh):
    placed = (
        P(None, ("seg", "dom")),
        P(None, ("seg", "dom")),
        P(None, ("seg", "dom")),
        P(("seg", "dom")),
        P(("seg", "dom")),
        P(("seg", "dom")),
        P(None, ("seg", "dom")),
        P(None, ("seg", "dom")),
        P(None, ("seg", "dom")),
        P(None, ("seg", "dom")),
        P(),
        P(),
        P(),
        P(),
        P(),
    )
    return jax.shard_map(
        shards,
        mesh=mesh,
        in_specs=placed,
        out_specs=(P(None, ("seg", "dom")), P(None, ("seg", "dom"))),
        check_vma=False,
    )
```

```python
import functools

import jax
import jax.numpy as jnp
from jax import lax
from jax.experimental import pallas as pl
from jax.experimental.pallas import tpu as pltpu
from jax.sharding import PartitionSpec as P

STEPS = 2
NEWTON = 4
IMPEDANCE = 1.0
FRICTION_A = 0.2
REGULARIZE = 0.25
TIME_STEP = 0.25

F32 = jnp.float32
BF16 = jnp.bfloat16

VALUES = 180
TRACE = 30
ROWS = 32
ELEMS = 1536
PEERS = 32
SLOTS = 128
POINTS = 16
NODES = 10
BLOCK = 256
TILES = ELEMS // BLOCK
LOCAL = 4 * TILES
REMOTE = PEERS * SLOTS // BLOCK
FAULTS = 2 * SLOTS
PARTS = 6
WIDTH = ELEMS // PARTS
CONSTANTS = ROWS + 2 * POINTS + 8
SEND_CHUNK = 24
REMOTE_CHUNK = 8
LOCAL_CHUNK = 24
VMEM_LIMIT = 32 * 2**20


def inverse_sinh(value):
    return jnp.log(value + jnp.sqrt(value * value + 1.0))


def row_order():
    row = lax.broadcasted_iota(jnp.int32, (4 * ROWS, 4 * TRACE), 0)
    column = lax.broadcasted_iota(jnp.int32, (4 * ROWS, 4 * TRACE), 1)
    face = lax.shift_right_logical(row, 5)
    value = jnp.bitwise_and(row, ROWS - 1)
    return jnp.where(column == 4 * value + face, 1.0, 0.0).astype(BF16)


def make_traces(packed, ordered, table, first, tiles):
    made = jnp.dot(ordered, packed, preferred_element_type=F32).astype(BF16)
    for face in range(4):
        for tile in range(tiles):
            start = (face * TILES + first + tile) * ROWS
            table[start : start + ROWS, :] = made[face * ROWS : (face + 1) * ROWS, tile * BLOCK : (tile + 1) * BLOCK]


def order_rows(order, restriction):
    return lax.dot_general(order, restriction, (((1,), (1,)), ((), ())), preferred_element_type=F32).astype(BF16)


def pick(table, index, first, blocks, chunk):
    width = index.shape[1]
    low = jnp.bitwise_and(index, BLOCK - 1)
    high = jnp.broadcast_to(lax.shift_right_arithmetic(index, 8), (8, width))
    lanes = lax.broadcasted_iota(jnp.int32, (BLOCK, width), 0)
    selector = jnp.where(lanes == low, 1.0, 0.0).astype(BF16)
    picked = jnp.zeros((ROWS // 8, 8, width), F32)
    for part in range(0, blocks, chunk):
        start = (first + part) * ROWS
        product = jnp.dot(table[start : start + chunk * ROWS, :], selector, preferred_element_type=F32)
        product = product.reshape(chunk, ROWS // 8, 8, width)
        for block in range(chunk):
            here = jnp.broadcast_to((high == first + part + block)[None], picked.shape)
            picked = jnp.where(here, product[block], picked)
    return picked.reshape(ROWS, width)


def pick_sent(table, send_faces, plus_faces, minus_faces, sent, plus_out, minus_out):
    index = jnp.concatenate([plus_faces[...], minus_faces[...]], axis=1)
    picked = pick(table, index, 0, LOCAL, SEND_CHUNK).astype(BF16)
    plus_out[...] = picked[:, :SLOTS]
    minus_out[...] = picked[:, SLOTS:]
    for pair in range(0, PEERS, 2):
        index = jnp.concatenate([send_faces[pair : pair + 1, :], send_faces[pair + 1 : pair + 2, :]], axis=1)
        picked = pick(table, index, 0, LOCAL, SEND_CHUNK).astype(BF16)
        sent[pair] = picked[:, :SLOTS]
        sent[pair + 1] = picked[:, SLOTS:]


def friction(difference, stress, state, to_points, to_nodes, jump):
    weights = [jnp.broadcast_to(to_points[:, n : n + 1], stress.shape) for n in range(NODES)]
    at_points = []
    for component in range(3):
        total = weights[0] * difference[component * NODES : component * NODES + 1]
        for n in range(1, NODES):
            row = component * NODES + n
            total = total + weights[n] * difference[row : row + 1]
        at_points.append(total)
    magnitude = jnp.sqrt(at_points[1] * at_points[1] + at_points[2] * at_points[2] + REGULARIZE)
    rate_scale = 0.5 * jnp.exp(state)
    slip_rate = jnp.zeros_like(magnitude)
    for _ in range(NEWTON):
        scaled_rate = slip_rate * rate_scale
        residual_value = IMPEDANCE * (magnitude - slip_rate) - stress * FRICTION_A * inverse_sinh(scaled_rate)
        derivative = IMPEDANCE + stress * FRICTION_A * rate_scale / jnp.sqrt(1.0 + scaled_rate * scaled_rate)
        slip_rate = slip_rate + residual_value / derivative
    share = slip_rate / magnitude
    point_jump = [at_points[0], at_points[1] * share, at_points[2] * share]
    columns = [jnp.broadcast_to(to_nodes[:, q : q + 1], (NODES, stress.shape[1])) for q in range(POINTS)]
    for component in range(3):
        total = columns[0] * point_jump[component][0:1]
        for q in range(1, POINTS):
            total = total + columns[q] * point_jump[component][q : q + 1]
        jump[component * NODES : (component + 1) * NODES, :] = total
    return slip_rate


def order_kernel(order):
    order[...] = row_order()


def first_kernel(
    order, element_state, send_faces, plus_faces, minus_faces, stress, state_variable, fault_count, restriction,
    sent, own_plus, plus_out, minus_out, table,
):
    make_traces(element_state[...].astype(BF16), order_rows(order[...], restriction[...]), table, 0, TILES)
    plus_out[ROWS : ROWS + POINTS, :] = stress[...]
    plus_out[ROWS + POINTS : ROWS + 2 * POINTS, :] = state_variable[...]
    plus_out[ROWS + 2 * POINTS :, :] = jnp.full((8, SLOTS), fault_count[0], jnp.int32).astype(F32)
    pick_sent(table, send_faces, plus_faces, minus_faces, sent, own_plus, minus_out)
    plus_out[0:ROWS, :] = own_plus[...].astype(F32)


def early_kernel(
    element_state, table, face_source, geometry, volume_ops, base_out, difference, state, base, sems,
):
    state_copy = pltpu.make_async_copy(element_state, state, sems.at[0])
    state_copy.start()

    def take(face):
        rows = slice(face * ROWS, (face + 1) * ROWS)
        for tile in range(TILES):
            columns = slice(tile * BLOCK, (tile + 1) * BLOCK)
            start = (face * TILES + tile) * ROWS
            own = table[start : start + ROWS, :].astype(F32)
            difference[rows, columns] = own - pick(table, face_source[face : face + 1, columns], 0, LOCAL, LOCAL_CHUNK)

    take(0)
    take(1)
    state_copy.wait()
    packed = state[...].astype(BF16)
    operators = volume_ops[...].astype(F32).T
    change = None
    for direction in range(3):
        operator = operators[direction * VALUES : (direction + 1) * VALUES].astype(BF16)
        term = jnp.dot(operator, packed, preferred_element_type=F32) * geometry[direction : direction + 1, :]
        change = term if change is None else change + term
    base[...] = state[...] + TIME_STEP * change
    base_copy = pltpu.make_async_copy(base, base_out, sems.at[1])
    base_copy.start()
    take(2)
    take(3)
    base_copy.wait()


def fault_kernel(
    difference, partner, next_plus, next_constants, face_source, plus_faces, minus_faces, own_plus, own_minus,
    fault_count, stress, state_variable, to_points, to_nodes, plain, index_out, slip_out, jump, masked,
):
    plus_side = jnp.concatenate([own_plus[...].astype(F32), next_plus[0:ROWS, :].astype(F32)], axis=1)
    minus_side = jnp.concatenate([partner[...].astype(F32), own_minus[...].astype(F32)], axis=1)
    both_stress = jnp.concatenate([stress[...], next_constants[ROWS : ROWS + POINTS, :]], axis=1)
    both_state = jnp.concatenate([state_variable[...], next_constants[ROWS + POINTS : ROWS + 2 * POINTS, :]], axis=1)
    slip_rate = friction(plus_side - minus_side, both_stress, both_state, to_points[...], to_nodes[...], jump)
    slot = lax.broadcasted_iota(jnp.int32, (1, SLOTS), 1)
    own_live = slot < fault_count[0]
    next_live = slot.astype(F32) < next_constants[ROWS + 2 * POINTS : ROWS + 2 * POINTS + 1, :]
    sign = jnp.concatenate([jnp.where(own_live, 1.0, 0.0), jnp.where(next_live, -1.0, 0.0)], axis=1)
    slip_out[...] = jnp.where(own_live, slip_rate[:, :SLOTS], 0.0)

    row = lax.broadcasted_iota(jnp.int32, (ROWS, FAULTS), 0)
    jump[TRACE : TRACE + 2, :] = jnp.zeros((2, FAULTS), F32)
    values = jnp.where(row < TRACE, jump[...] * sign, jnp.where(row == TRACE, jnp.abs(sign), 0.0))
    coarse = values.astype(BF16).astype(F32)
    parts = jnp.concatenate([coarse, values - coarse], axis=0)
    faces = jnp.concatenate([plus_faces[...], minus_faces[...]], axis=1)
    high = jnp.broadcast_to(lax.shift_right_logical(faces, 8), parts.shape)
    for block in range(LOCAL):
        masked[block * 2 * ROWS : (block + 1) * 2 * ROWS, :] = jnp.where(high == block, parts, 0.0).astype(BF16)
    lanes = lax.broadcasted_iota(jnp.int32, (BLOCK, FAULTS), 0)
    selector = jnp.where(lanes == jnp.bitwise_and(faces, BLOCK - 1), 1.0, 0.0).astype(BF16)
    changed = lax.dot_general(masked[...], selector, (((1,), (1,)), ((), ())), preferred_element_type=F32)
    for face in range(4):
        rows = slice(face * ROWS, (face + 1) * ROWS)
        for tile in range(TILES):
            columns = slice(tile * BLOCK, (tile + 1) * BLOCK)
            start = (face * TILES + tile) * 2 * ROWS
            value = changed[start : start + ROWS, :] + changed[start + ROWS : start + 2 * ROWS, :]
            here = value[TRACE : TRACE + 1] > 0.5
            plain[rows, columns] = jnp.where(here, value, difference[rows, columns])
            index_out[face : face + 1, columns] = jnp.where(
                here, -1, face_source[face : face + 1, columns] - 4 * ELEMS
            )


def step_kernel(
    last, order, base_in, plain, received, index, face_area, restriction, lift_operator, send_faces, plus_faces,
    minus_faces, *rest,
):
    if last:
        state_out, arrived, scaled, base, state, sems = rest
    else:
        state_out, sent, plus_out, minus_out, table, arrived, scaled, base, state, sems = rest
    base_copy = pltpu.make_async_copy(base_in, base, sems.at[PARTS])
    base_copy.start()
    for block in range(REMOTE):
        arrived[block * ROWS : (block + 1) * ROWS, :] = jnp.concatenate(
            [received[2 * block], received[2 * block + 1]], axis=1
        )
    lift = lax.dot_general(
        lift_operator[...], order[...], (((1,), (1,)), ((), ())), preferred_element_type=F32
    ).astype(BF16)
    for face in range(4):
        if last and face == 3:
            base_copy.wait()
        rows = slice(face * ROWS, (face + 1) * ROWS)
        for tile in range(TILES):
            columns = slice(tile * BLOCK, (tile + 1) * BLOCK)
            face_jump = plain[rows, columns] - pick(
                arrived, index[face : face + 1, columns], 0, REMOTE, REMOTE_CHUNK
            )
            scaled[rows, columns] = (face_jump * face_area[face : face + 1, columns]).astype(BF16)
    if not last:
        base_copy.wait()
    leaving = []
    for part in range(PARTS):
        columns = slice(part * WIDTH, (part + 1) * WIDTH)
        lifted = jnp.dot(lift, scaled[:, columns], preferred_element_type=F32)
        state[:, columns] = base[:, columns] - TIME_STEP * lifted
        leaving.append(pltpu.make_async_copy(state.at[:, columns], state_out.at[:, columns], sems.at[part]))
        leaving[-1].start()
    if not last:
        make_traces(state[...].astype(BF16), order_rows(order[...], restriction[...]), table, 0, TILES)
        pick_sent(table, send_faces, plus_faces, minus_faces, sent, plus_out, minus_out)
    for copy in leaving:
        copy.wait()


VMEM = pl.BlockSpec(memory_space=pltpu.VMEM)
SMEM = pl.BlockSpec(memory_space=pltpu.SMEM)
HBM = pl.BlockSpec(memory_space=pltpu.HBM)


def call(kernel, name, args, specs, outs, out_specs, scratch, flops):
    return pl.pallas_call(
        kernel,
        out_shape=[
            pltpu.HBM(shape, dtype) if spec is HBM else jax.ShapeDtypeStruct(shape, dtype)
            for (shape, dtype), spec in zip(outs, out_specs, strict=True)
        ],
        in_specs=specs,
        out_specs=out_specs,
        scratch_shapes=scratch,
        compiler_params=pltpu.CompilerParams(vmem_limit_bytes=VMEM_LIMIT),
        cost_estimate=pl.CostEstimate(flops=flops, bytes_accessed=4 * 2**20, transcendentals=0),
        name=name,
    )(*[pltpu.with_memory_space_constraint(a, pltpu.HBM) if s is HBM else a for a, s in zip(args, specs, strict=True)])


def shards(
    element_state,
    face_source,
    send_faces,
    plus_faces,
    minus_faces,
    fault_count,
    normal_stress,
    state_variable,
    geometry,
    face_area,
    restriction,
    volume_ops,
    lift_operator,
    to_points,
    to_nodes,
):
    segments = lax.axis_size("seg")
    up = [(s, (s + 1) % segments) for s in range(segments)]
    down = [(s, (s - 1) % segments) for s in range(segments)]
    plus_faces = plus_faces.reshape(1, SLOTS)
    minus_faces = minus_faces.reshape(1, SLOTS)
    restriction = restriction.T
    volume_ops = volume_ops.T
    side = ((ROWS, SLOTS), BF16)
    sent_shape = ((PEERS, ROWS, SLOTS), BF16)
    table_shape = ((LOCAL * ROWS, BLOCK), BF16)
    state_shape = (element_state.shape, F32)
    (order,) = call(order_kernel, "order", (), [], [((4 * ROWS, 4 * TRACE), BF16)], [VMEM], [], 4 * 10**9)
    sent, own_plus, plus, minus, table = call(
        first_kernel,
        "first",
        (
            order, element_state, send_faces, plus_faces, minus_faces, normal_stress, state_variable, fault_count,
            restriction,
        ),
        [VMEM] * 7 + [SMEM, VMEM],
        [sent_shape, side, ((CONSTANTS, SLOTS), F32), side, table_shape],
        [VMEM] * 5,
        [],
        2 * 10**9,
    )
    next_constants = None
    for step in range(STEPS):
        last = step == STEPS - 1
        received = lax.all_to_all(sent, "dom", 0, 0, tiled=True)
        partner = lax.ppermute(minus, "seg", up)
        next_plus = lax.ppermute(plus, "seg", down)
        next_constants = next_plus if next_constants is None else next_constants
        base, difference = call(
            early_kernel,
            "early",
            (element_state, table, face_source, geometry, volume_ops),
            [HBM] + [VMEM] * 4,
            [state_shape, ((4 * ROWS, ELEMS), F32)],
            [HBM, VMEM],
            [pltpu.VMEM(*state_shape), pltpu.VMEM(*state_shape), pltpu.SemaphoreType.DMA((2,))],
            2 * 10**9,
        )
        plain, index, slip = call(
            fault_kernel,
            "fault",
            (
                difference, partner, next_plus, next_constants, face_source, plus_faces, minus_faces, own_plus, minus,
                fault_count, normal_stress, state_variable, to_points, to_nodes,
            ),
            [VMEM] * 9 + [SMEM] + [VMEM] * 4,
            [((4 * ROWS, ELEMS), F32), (face_source.shape, jnp.int32), (normal_stress.shape, F32)],
            [VMEM] * 3,
            [pltpu.VMEM((ROWS, FAULTS), F32), pltpu.VMEM((LOCAL * 2 * ROWS, FAULTS), BF16)],
            10**9,
        )
        args = (
            order, base, plain, received, index, face_area, restriction, lift_operator, send_faces, plus_faces,
            minus_faces,
        )
        specs = [VMEM, HBM] + [VMEM] * 9
        scratch = [
            pltpu.VMEM((REMOTE * ROWS, BLOCK), BF16),
            pltpu.VMEM((4 * ROWS, ELEMS), BF16),
            pltpu.VMEM(*state_shape),
            pltpu.VMEM(*state_shape),
            pltpu.SemaphoreType.DMA((PARTS + 1,)),
        ]
        kernel = functools.partial(step_kernel, last)
        if last:
            (element_state,) = call(kernel, "last", args, specs, [state_shape], [HBM], scratch, 4 * 10**9)
            return element_state, slip
        outs = [state_shape, sent_shape, side, side, table_shape]
        element_state, sent, own_plus, minus, table = call(
            kernel, "step", args, specs, outs, [HBM, VMEM, VMEM, VMEM, VMEM], scratch, 4 * 10**9
        )
        plus = own_plus


def solution(mesh):
    placed = (
        P(None, ("seg", "dom")),
        P(None, ("seg", "dom")),
        P(None, ("seg", "dom")),
        P(("seg", "dom")),
        P(("seg", "dom")),
        P(("seg", "dom")),
        P(None, ("seg", "dom")),
        P(None, ("seg", "dom")),
        P(None, ("seg", "dom")),
        P(None, ("seg", "dom")),
        P(),
        P(),
        P(),
        P(),
        P(),
    )
    return jax.shard_map(
        shards,
        mesh=mesh,
        in_specs=placed,
        out_specs=(P(None, ("seg", "dom")), P(None, ("seg", "dom"))),
        check_vma=False,
    )
```

```python
import functools

import jax
import jax.numpy as jnp
from jax import lax
from jax.experimental import pallas as pl
from jax.experimental.pallas import tpu as pltpu
from jax.sharding import PartitionSpec as P

STEPS = 2
NEWTON = 4
IMPEDANCE = 1.0
FRICTION_A = 0.2
REGULARIZE = 0.25
TIME_STEP = 0.25

F32 = jnp.float32
BF16 = jnp.bfloat16

VALUES = 180
TRACE = 30
ROWS = 32
ELEMS = 1536
PEERS = 32
SLOTS = 128
POINTS = 16
NODES = 10
BLOCK = 256
TILES = ELEMS // BLOCK
LOCAL = 4 * TILES
REMOTE = PEERS * SLOTS // BLOCK
ROTATE = 22
FAULTS = 2 * SLOTS
PARTS = 6
ORDER = [(i + ROTATE) % PEERS for i in range(PEERS)]
WIDTH = ELEMS // PARTS
CONSTANTS = ROWS + 2 * POINTS + 8
SEND_CHUNK = 24
REMOTE_CHUNK = 8
LOCAL_CHUNK = 24
VMEM_LIMIT = 32 * 2**20


def inverse_sinh(value):
    return jnp.log(value + jnp.sqrt(value * value + 1.0))


def row_order():
    row = lax.broadcasted_iota(jnp.int32, (4 * ROWS, 4 * TRACE), 0)
    column = lax.broadcasted_iota(jnp.int32, (4 * ROWS, 4 * TRACE), 1)
    face = lax.shift_right_logical(row, 5)
    value = jnp.bitwise_and(row, ROWS - 1)
    return jnp.where(column == 4 * value + face, 1.0, 0.0).astype(BF16)


def make_traces(packed, ordered, table, first, tiles):
    made = jnp.dot(ordered, packed, preferred_element_type=F32).astype(BF16)
    for face in range(4):
        for tile in range(tiles):
            start = (face * TILES + first + tile) * ROWS
            table[start : start + ROWS, :] = made[face * ROWS : (face + 1) * ROWS, tile * BLOCK : (tile + 1) * BLOCK]


def order_rows(order, restriction):
    return lax.dot_general(order, restriction, (((1,), (1,)), ((), ())), preferred_element_type=F32).astype(BF16)


def pick(table, index, first, blocks, chunk):
    width = index.shape[1]
    low = jnp.bitwise_and(index, BLOCK - 1)
    high = jnp.broadcast_to(lax.shift_right_arithmetic(index, 8), (8, width))
    lanes = lax.broadcasted_iota(jnp.int32, (BLOCK, width), 0)
    selector = jnp.where(lanes == low, 1.0, 0.0).astype(BF16)
    picked = jnp.zeros((ROWS // 8, 8, width), F32)
    for part in range(0, blocks, chunk):
        start = (first + part) * ROWS
        product = jnp.dot(table[start : start + chunk * ROWS, :], selector, preferred_element_type=F32)
        product = product.reshape(chunk, ROWS // 8, 8, width)
        for block in range(chunk):
            here = jnp.broadcast_to((high == first + part + block)[None], picked.shape)
            picked = jnp.where(here, product[block], picked)
    return picked.reshape(ROWS, width)


def pick_sent(table, send_faces, plus_faces, minus_faces, sent, plus_out, minus_out):
    index = jnp.concatenate([plus_faces[...], minus_faces[...]], axis=1)
    picked = pick(table, index, 0, LOCAL, SEND_CHUNK).astype(BF16)
    plus_out[...] = picked[:, :SLOTS]
    minus_out[...] = picked[:, SLOTS:]
    for pair in range(0, PEERS, 2):
        index = jnp.concatenate([send_faces[peer : peer + 1, :] for peer in ORDER[pair : pair + 2]], axis=1)
        picked = pick(table, index, 0, LOCAL, SEND_CHUNK).astype(BF16)
        sent[pair] = picked[:, :SLOTS]
        sent[pair + 1] = picked[:, SLOTS:]


def friction(difference, stress, state, to_points, to_nodes, jump):
    weights = [jnp.broadcast_to(to_points[:, n : n + 1], stress.shape) for n in range(NODES)]
    at_points = []
    for component in range(3):
        total = weights[0] * difference[component * NODES : component * NODES + 1]
        for n in range(1, NODES):
            row = component * NODES + n
            total = total + weights[n] * difference[row : row + 1]
        at_points.append(total)
    magnitude = jnp.sqrt(at_points[1] * at_points[1] + at_points[2] * at_points[2] + REGULARIZE)
    rate_scale = 0.5 * jnp.exp(state)
    slip_rate = jnp.zeros_like(magnitude)
    for _ in range(NEWTON):
        scaled_rate = slip_rate * rate_scale
        residual_value = IMPEDANCE * (magnitude - slip_rate) - stress * FRICTION_A * inverse_sinh(scaled_rate)
        derivative = IMPEDANCE + stress * FRICTION_A * rate_scale / jnp.sqrt(1.0 + scaled_rate * scaled_rate)
        slip_rate = slip_rate + residual_value / derivative
    share = slip_rate / magnitude
    point_jump = [at_points[0], at_points[1] * share, at_points[2] * share]
    columns = [jnp.broadcast_to(to_nodes[:, q : q + 1], (NODES, stress.shape[1])) for q in range(POINTS)]
    for component in range(3):
        total = columns[0] * point_jump[component][0:1]
        for q in range(1, POINTS):
            total = total + columns[q] * point_jump[component][q : q + 1]
        jump[component * NODES : (component + 1) * NODES, :] = total
    return slip_rate


def order_kernel(order):
    order[...] = row_order()


def first_kernel(
    order, element_state, send_faces, plus_faces, minus_faces, stress, state_variable, fault_count, restriction,
    sent, own_plus, plus_out, minus_out, table,
):
    make_traces(element_state[...].astype(BF16), order_rows(order[...], restriction[...]), table, 0, TILES)
    plus_out[ROWS : ROWS + POINTS, :] = stress[...]
    plus_out[ROWS + POINTS : ROWS + 2 * POINTS, :] = state_variable[...]
    plus_out[ROWS + 2 * POINTS :, :] = jnp.full((8, SLOTS), fault_count[0], jnp.int32).astype(F32)
    pick_sent(table, send_faces, plus_faces, minus_faces, sent, own_plus, minus_out)
    plus_out[0:ROWS, :] = own_plus[...].astype(F32)


def early_kernel(
    element_state, table, face_source, geometry, volume_ops, base_out, difference, state, base, sems,
):
    state_copy = pltpu.make_async_copy(element_state, state, sems.at[0])
    state_copy.start()

    def take(face):
        rows = slice(face * ROWS, (face + 1) * ROWS)
        for tile in range(TILES):
            columns = slice(tile * BLOCK, (tile + 1) * BLOCK)
            start = (face * TILES + tile) * ROWS
            own = table[start : start + ROWS, :].astype(F32)
            difference[rows, columns] = own - pick(table, face_source[face : face + 1, columns], 0, LOCAL, LOCAL_CHUNK)

    take(0)
    take(1)
    state_copy.wait()
    packed = state[...].astype(BF16)
    operators = volume_ops[...].astype(F32).T
    change = None
    for direction in range(3):
        operator = operators[direction * VALUES : (direction + 1) * VALUES].astype(BF16)
        term = jnp.dot(operator, packed, preferred_element_type=F32) * geometry[direction : direction + 1, :]
        change = term if change is None else change + term
    base[...] = state[...] + TIME_STEP * change
    base_copy = pltpu.make_async_copy(base, base_out, sems.at[1])
    base_copy.start()
    take(2)
    take(3)
    base_copy.wait()


def fault_kernel(
    difference, partner, next_plus, next_constants, face_source, plus_faces, minus_faces, own_plus, own_minus,
    fault_count, stress, state_variable, to_points, to_nodes, plain, index_out, slip_out, jump, masked,
):
    plus_side = jnp.concatenate([own_plus[...].astype(F32), next_plus[0:ROWS, :].astype(F32)], axis=1)
    minus_side = jnp.concatenate([partner[...].astype(F32), own_minus[...].astype(F32)], axis=1)
    both_stress = jnp.concatenate([stress[...], next_constants[ROWS : ROWS + POINTS, :]], axis=1)
    both_state = jnp.concatenate([state_variable[...], next_constants[ROWS + POINTS : ROWS + 2 * POINTS, :]], axis=1)
    slip_rate = friction(plus_side - minus_side, both_stress, both_state, to_points[...], to_nodes[...], jump)
    slot = lax.broadcasted_iota(jnp.int32, (1, SLOTS), 1)
    own_live = slot < fault_count[0]
    next_live = slot.astype(F32) < next_constants[ROWS + 2 * POINTS : ROWS + 2 * POINTS + 1, :]
    sign = jnp.concatenate([jnp.where(own_live, 1.0, 0.0), jnp.where(next_live, -1.0, 0.0)], axis=1)
    slip_out[...] = jnp.where(own_live, slip_rate[:, :SLOTS], 0.0)

    row = lax.broadcasted_iota(jnp.int32, (ROWS, FAULTS), 0)
    jump[TRACE : TRACE + 2, :] = jnp.zeros((2, FAULTS), F32)
    values = jnp.where(row < TRACE, jump[...] * sign, jnp.where(row == TRACE, jnp.abs(sign), 0.0))
    coarse = values.astype(BF16).astype(F32)
    parts = jnp.concatenate([coarse, values - coarse], axis=0)
    faces = jnp.concatenate([plus_faces[...], minus_faces[...]], axis=1)
    high = jnp.broadcast_to(lax.shift_right_logical(faces, 8), parts.shape)
    for block in range(LOCAL):
        masked[block * 2 * ROWS : (block + 1) * 2 * ROWS, :] = jnp.where(high == block, parts, 0.0).astype(BF16)
    lanes = lax.broadcasted_iota(jnp.int32, (BLOCK, FAULTS), 0)
    selector = jnp.where(lanes == jnp.bitwise_and(faces, BLOCK - 1), 1.0, 0.0).astype(BF16)
    changed = lax.dot_general(masked[...], selector, (((1,), (1,)), ((), ())), preferred_element_type=F32)
    for face in range(4):
        rows = slice(face * ROWS, (face + 1) * ROWS)
        for tile in range(TILES):
            columns = slice(tile * BLOCK, (tile + 1) * BLOCK)
            start = (face * TILES + tile) * 2 * ROWS
            value = changed[start : start + ROWS, :] + changed[start + ROWS : start + 2 * ROWS, :]
            here = value[TRACE : TRACE + 1] > 0.5
            plain[rows, columns] = jnp.where(here, value, difference[rows, columns])
            index_out[face : face + 1, columns] = jnp.where(
                here, -1, face_source[face : face + 1, columns] - 4 * ELEMS
            )


def step_kernel(
    last, order, base_in, plain, received, index, face_area, restriction, lift_operator, send_faces, plus_faces,
    minus_faces, *rest,
):
    if last:
        state_out, arrived, scaled, base, state, sems = rest
    else:
        state_out, sent, plus_out, minus_out, table, arrived, scaled, base, state, sems = rest
    base_copy = pltpu.make_async_copy(base_in, base, sems.at[PARTS])
    base_copy.start()
    for block in range(REMOTE):
        arrived[block * ROWS : (block + 1) * ROWS, :] = jnp.concatenate(
            [received[ORDER.index(peer)] for peer in (2 * block, 2 * block + 1)], axis=1
        )
    lift = lax.dot_general(
        lift_operator[...], order[...], (((1,), (1,)), ((), ())), preferred_element_type=F32
    ).astype(BF16)
    for face in range(4):
        if last and face == 3:
            base_copy.wait()
        rows = slice(face * ROWS, (face + 1) * ROWS)
        for tile in range(TILES):
            columns = slice(tile * BLOCK, (tile + 1) * BLOCK)
            face_jump = plain[rows, columns] - pick(
                arrived, index[face : face + 1, columns], 0, REMOTE, REMOTE_CHUNK
            )
            scaled[rows, columns] = (face_jump * face_area[face : face + 1, columns]).astype(BF16)
    if not last:
        base_copy.wait()
    leaving = []
    for part in range(PARTS):
        columns = slice(part * WIDTH, (part + 1) * WIDTH)
        lifted = jnp.dot(lift, scaled[:, columns], preferred_element_type=F32)
        state[:, columns] = base[:, columns] - TIME_STEP * lifted
        leaving.append(pltpu.make_async_copy(state.at[:, columns], state_out.at[:, columns], sems.at[part]))
        leaving[-1].start()
    if not last:
        make_traces(state[...].astype(BF16), order_rows(order[...], restriction[...]), table, 0, TILES)
        pick_sent(table, send_faces, plus_faces, minus_faces, sent, plus_out, minus_out)
    for copy in leaving:
        copy.wait()


VMEM = pl.BlockSpec(memory_space=pltpu.VMEM)
SMEM = pl.BlockSpec(memory_space=pltpu.SMEM)
HBM = pl.BlockSpec(memory_space=pltpu.HBM)


def call(kernel, name, args, specs, outs, out_specs, scratch, flops):
    return pl.pallas_call(
        kernel,
        out_shape=[
            pltpu.HBM(shape, dtype) if spec is HBM else jax.ShapeDtypeStruct(shape, dtype)
            for (shape, dtype), spec in zip(outs, out_specs, strict=True)
        ],
        in_specs=specs,
        out_specs=out_specs,
        scratch_shapes=scratch,
        compiler_params=pltpu.CompilerParams(vmem_limit_bytes=VMEM_LIMIT),
        cost_estimate=pl.CostEstimate(flops=flops, bytes_accessed=4 * 2**20, transcendentals=0),
        name=name,
    )(*[pltpu.with_memory_space_constraint(a, pltpu.HBM) if s is HBM else a for a, s in zip(args, specs, strict=True)])


def shards(
    element_state,
    face_source,
    send_faces,
    plus_faces,
    minus_faces,
    fault_count,
    normal_stress,
    state_variable,
    geometry,
    face_area,
    restriction,
    volume_ops,
    lift_operator,
    to_points,
    to_nodes,
):
    segments = lax.axis_size("seg")
    up = [(s, (s + 1) % segments) for s in range(segments)]
    down = [(s, (s - 1) % segments) for s in range(segments)]
    plus_faces = plus_faces.reshape(1, SLOTS)
    minus_faces = minus_faces.reshape(1, SLOTS)
    restriction = restriction.T
    volume_ops = volume_ops.T
    side = ((ROWS, SLOTS), BF16)
    sent_shape = ((PEERS, ROWS, SLOTS), BF16)
    table_shape = ((LOCAL * ROWS, BLOCK), BF16)
    state_shape = (element_state.shape, F32)
    (order,) = call(order_kernel, "order", (), [], [((4 * ROWS, 4 * TRACE), BF16)], [VMEM], [], 4 * 10**9)
    sent, own_plus, plus, minus, table = call(
        first_kernel,
        "first",
        (
            order, element_state, send_faces, plus_faces, minus_faces, normal_stress, state_variable, fault_count,
            restriction,
        ),
        [VMEM] * 7 + [SMEM, VMEM],
        [sent_shape, side, ((CONSTANTS, SLOTS), F32), side, table_shape],
        [VMEM] * 5,
        [],
        2 * 10**9,
    )
    next_constants = None
    for step in range(STEPS):
        last = step == STEPS - 1
        received = lax.all_to_all(sent, "dom", 0, 0, axis_index_groups=[ORDER], tiled=True)
        partner = lax.ppermute(minus, "seg", up)
        next_plus = lax.ppermute(plus, "seg", down)
        next_constants = next_plus if next_constants is None else next_constants
        base, difference = call(
            early_kernel,
            "early",
            (element_state, table, face_source, geometry, volume_ops),
            [HBM] + [VMEM] * 4,
            [state_shape, ((4 * ROWS, ELEMS), F32)],
            [HBM, VMEM],
            [pltpu.VMEM(*state_shape), pltpu.VMEM(*state_shape), pltpu.SemaphoreType.DMA((2,))],
            2 * 10**9,
        )
        plain, index, slip = call(
            fault_kernel,
            "fault",
            (
                difference, partner, next_plus, next_constants, face_source, plus_faces, minus_faces, own_plus, minus,
                fault_count, normal_stress, state_variable, to_points, to_nodes,
            ),
            [VMEM] * 9 + [SMEM] + [VMEM] * 4,
            [((4 * ROWS, ELEMS), F32), (face_source.shape, jnp.int32), (normal_stress.shape, F32)],
            [VMEM] * 3,
            [pltpu.VMEM((ROWS, FAULTS), F32), pltpu.VMEM((LOCAL * 2 * ROWS, FAULTS), BF16)],
            10**9,
        )
        args = (
            order, base, plain, received, index, face_area, restriction, lift_operator, send_faces, plus_faces,
            minus_faces,
        )
        specs = [VMEM, HBM] + [VMEM] * 9
        scratch = [
            pltpu.VMEM((REMOTE * ROWS, BLOCK), BF16),
            pltpu.VMEM((4 * ROWS, ELEMS), BF16),
            pltpu.VMEM(*state_shape),
            pltpu.VMEM(*state_shape),
            pltpu.SemaphoreType.DMA((PARTS + 1,)),
        ]
        kernel = functools.partial(step_kernel, last)
        if last:
            (element_state,) = call(kernel, "last", args, specs, [state_shape], [HBM], scratch, 4 * 10**9)
            return element_state, slip
        outs = [state_shape, sent_shape, side, side, table_shape]
        element_state, sent, own_plus, minus, table = call(
            kernel, "step", args, specs, outs, [HBM, VMEM, VMEM, VMEM, VMEM], scratch, 4 * 10**9
        )
        plus = own_plus


def solution(mesh):
    placed = (
        P(None, ("seg", "dom")),
        P(None, ("seg", "dom")),
        P(None, ("seg", "dom")),
        P(("seg", "dom")),
        P(("seg", "dom")),
        P(("seg", "dom")),
        P(None, ("seg", "dom")),
        P(None, ("seg", "dom")),
        P(None, ("seg", "dom")),
        P(None, ("seg", "dom")),
        P(),
        P(),
        P(),
        P(),
        P(),
    )
    return jax.shard_map(
        shards,
        mesh=mesh,
        in_specs=placed,
        out_specs=(P(None, ("seg", "dom")), P(None, ("seg", "dom"))),
        check_vma=False,
    )
```
